128 devices in a mesh: tm: 8 (over x_lo, y), gx: 4 (over x_hi, core), gy: 4 (over z).
Axes of the slice: x: 4 (x_hi: 2, x_lo: 2; x = x_hi * 2 + x_lo), y: 4, z: 4, core: 2. Of those that a mesh axis runs over, the one named last changes fastest.
Arguments:
- guess: float32 [3, 8, 64, 64, 256], P(None, 'tm', 'gx', 'gy'), may hold values from -1 to 1
Outputs:
- updated: float32 [3, 8, 64, 64, 256], P(None, 'tm', 'gx', 'gy')
The draws below stay inside these ranges and needn't reach their ends.
All inputs are finite; a program needn't handle non-finite values.
Results may differ from the reference program's by a relative error of at most 0.0001.
Values sent between devices are 32-bit elements; how exact they have to be, the bound alone decides.
A program may use at most 128 MiB of HBM per device.

```python
import jax
import jax.numpy as jnp

CZ = 256
NODES = 3
SLICES = 8
NX = 64
NY = 64
N_TM = 8


def level_of(stream_key, shape, pieces, smallest, top_value):
    level = 1.0
    for dim, blocks in pieces:
        draws = jax.random.uniform(jax.random.fold_in(jax.random.fold_in(stream_key, 6), dim), (blocks,), jnp.float32, smallest / len(pieces), top_value / len(pieces))
        level = level * jnp.repeat(jnp.exp(draws), shape[dim] // blocks).reshape((-1,) + (1,) * (len(shape) - 1 - dim))
    return level


def setup_inputs(seed: int = 0) -> dict:
    seeds = jax.random.split(jax.random.key(seed), 2)
    guess = jnp.clip(jax.random.uniform(seeds[0], (NODES, SLICES, NX, NY, CZ), jnp.float32, -1.0, 1.0) * level_of(seeds[0], (NODES, SLICES, NX, NY, CZ), ((1, 8), (2, 4), (3, 4)), -0.4, 0.0), -1.0, 1.0)
    return {"guess": guess}


KAPPA = 1.0
STEP = 0.01
HALF_STEP = 0.005
WEIGHTS = ((5.0 / 24.0, 1.0 / 3.0, -1.0 / 24.0), (-1.0 / 24.0, 1.0 / 3.0, 5.0 / 24.0))


def laplace(field, inverse):
    beside = jnp.roll(field, -1, 0) + jnp.roll(field, 1, 0)
    beside = beside + jnp.roll(field, -1, 1) + jnp.roll(field, 1, 1)
    beside = beside + jnp.roll(field, -1, 2) + jnp.roll(field, 1, 2)
    return (beside - 6.0 * field) * inverse


def tendency(values, inverse):
    potential = values * values * values - values - KAPPA * laplace(values, inverse)
    return laplace(potential, inverse)


def integrals(forces):
    return [STEP * (WEIGHTS[node][0] * forces[0] + WEIGHTS[node][1] * forces[1] + WEIGHTS[node][2] * forces[2]) for node in range(2)]


def sdc_sweep(start, old_forces, parts, inverse):
    nodes = [start]
    forces = []
    current = start
    for node in range(2):
        now = tendency(current, inverse)
        forces.append(now)
        current = current + HALF_STEP * (now - old_forces[node]) + parts[node]
        nodes.append(current)
    return nodes, forces


def restrict(field):
    sx, sy, sz = field.shape
    return jnp.mean(field.reshape(sx // 2, 2, sy // 2, 2, sz // 2, 2), axis=(1, 3, 5))


def prolong(field):
    sx, sy, sz = field.shape
    wide = jnp.broadcast_to(field[:, None, :, None, :, None], (sx, 2, sy, 2, sz, 2))
    return wide.reshape(sx * 2, sy * 2, sz * 2)


def reference(guess):
    results = []
    chain = None
    for slice_index in range(N_TM):
        nodes = [guess[j, slice_index] for j in range(3)]
        if slice_index == 0:
            start = guess[0, 0]
        else:
            start = guess[2, slice_index - 1]
        old = [tendency(v, 1.0) for v in nodes]
        first_nodes, first_forces = sdc_sweep(start, old, integrals(old), 1.0)
        old = first_forces + [tendency(first_nodes[2], 1.0)]
        second_nodes, second_forces = sdc_sweep(start, old, integrals(old), 1.0)
        fine_forces = second_forces + [tendency(second_nodes[2], 1.0)]
        coarse_nodes = [restrict(v) for v in second_nodes]
        coarse_parts = integrals([restrict(v) for v in fine_forces])
        coarse_old = [tendency(coarse_nodes[j], 0.25) for j in range(2)]
        if slice_index == 0:
            initial = coarse_nodes[0]
        else:
            initial = chain
        values, unused = sdc_sweep(initial, coarse_old, coarse_parts, 0.25)
        chain = values[2]
        results.append(jnp.stack([second_nodes[j] + prolong(values[j] - coarse_nodes[j]) for j in range(3)]))
    return jnp.stack(results, axis=1)
```

```python
import jax
import jax.numpy as jnp
import numpy as np
from jax import lax
from jax.experimental import pallas as pl
from jax.experimental.pallas import tpu as pltpu
from jax.sharding import PartitionSpec as P

DT = 0.01
HALF = 0.005
W = ((5.0 / 24.0, 1.0 / 3.0, -1.0 / 24.0), (-1.0 / 24.0, 1.0 / 3.0, 5.0 / 24.0))
OLD = (
    (DT * (W[0][0] - 0.5), DT * W[0][1], DT * W[0][2]),
    (DT * W[1][0], DT * (W[1][1] - 0.5), DT * W[1][2]),
)
MESH = pl.DeviceIdType.MESH
DIRS = ((1, 0), (-1, 0), (0, 1), (0, -1), (1, 1), (1, -1), (-1, 1), (-1, -1))
F32 = jnp.float32
HIGH = lax.Precision.HIGHEST


def dot(a, b):
    return jnp.dot(a, b, precision=HIGH, preferred_element_type=F32)


def around(c, low, high):
    rows, z = c.shape
    s = (low + high) + (pltpu.roll(c, 1, 0) + pltpu.roll(c, rows - 1, 0))
    s = s + (pltpu.roll(c, 1, 1) + pltpu.roll(c, z - 1, 1))
    return s - 6.0 * c


def around3(v):
    c = v[1:-1]
    rows, z = c.shape[1:]
    s = v[:-2] + v[2:] + pltpu.roll(c, 1, 1) + pltpu.roll(c, rows - 1, 1)
    s = s + pltpu.roll(c, 1, 2) + pltpu.roll(c, z - 1, 2)
    return s - 6.0 * c


def loop(count, body, unroll=2):
    def step(i, carry):
        body(i)
        return carry

    lax.fori_loop(0, count, step, 0, unroll=unroll)


def potential(src, mu, count):
    def body(x):
        c = src[x + 1]
        mu[x] = c * (c * c - 1.0) - around(c, src[x], src[x + 2])

    loop(count, body)


def edge(h, d):
    return pl.ds(16 - h, h) if d > 0 else pl.ds(0, h)


def halo(h, d, at):
    return pl.ds(at - h, h) if d > 0 else pl.ds(at + 16, h)


def kernel(
    g, zavg, zdup, ydup, out,
    raw, rsy, rry, rrc, q, mu, mu2,
    start, k0, k1, ksy, kry, krc,
    u11, u12, u21, bb, usy, ury, urc, u22,
    fs, f11, f21, j0, j1,
    pair, co, cb, xext, gath, v0, v1, m0, stage, back, half,
    st_s, st_r, raw_s, raw_r, k_s, k_r, s_s, s_r, u_s, u_r, g_s, g_r, b_s, b_r,
):
    n, a, b = lax.axis_index("tm"), lax.axis_index("gx"), lax.axis_index("gy")

    def at(dt, dx, dy):
        return (lax.rem(n + dt + 8, 8), lax.rem(a + dx + 4, 4), lax.rem(b + dy + 4, 4))

    barrier = pltpu.get_barrier_semaphore()
    for dx, dy in DIRS:
        pl.semaphore_signal(barrier, inc=1, device_id=at(0, dx, dy), device_id_type=MESH)
    for dt in range(1, 8):
        pl.semaphore_signal(barrier, inc=1, device_id=at(dt, 0, 0), device_id_type=MESH)
    pl.semaphore_wait(barrier, 15)

    def send(src, dst, ss, rs, to):
        copy = pltpu.make_async_remote_copy(
            src_ref=src, dst_ref=dst, send_sem=ss, recv_sem=rs, device_id=to, device_id_type=MESH
        )
        copy.start()
        return copy

    mid = start.at[pl.ds(6, 16), pl.ds(8, 16), :]
    along = pltpu.make_async_remote_copy(
        src_ref=g.at[2, 0], dst_ref=mid, send_sem=st_s, recv_sem=st_r,
        device_id=at(1, 0, 0), device_id_type=MESH,
    )

    @pl.when(n < 7)
    def _():
        along.start()

    for j in range(3):
        rsy[0, :, 2 * j : 2 * j + 2, :] = g[j, 0, :, 14:16, :]
        rsy[1, :, 2 * j : 2 * j + 2, :] = g[j, 0, :, 0:2, :]
    raws = []
    for k, (dx, dy) in enumerate(DIRS):
        if dy == 0:
            src = g.at[:, 0, edge(2, dx)]
            dst = raw.at[:, halo(2, dx, 2), pl.ds(8, 16), :]
        elif dx == 0:
            src, dst = rsy.at[(1 - dy) // 2], rry.at[(1 - dy) // 2]
        else:
            src, dst = rsy.at[(1 - dy) // 2, edge(1, dx)], rrc.at[k - 4]
        raws.append(send(src, dst, raw_s.at[k], raw_r.at[k], at(0, dx, dy)))
    raw[:, 2:18, 8:24, :] = g[:, 0]
    for copy in raws:
        copy.wait_recv()
    for s, row in ((0, 6), (1, 24)):
        for j in range(3):
            raw[j, 2:18, row : row + 2, :] = rry[s, :, 2 * j : 2 * j + 2, :]
            for e, x in ((0, 1), (2, 18)):
                raw[j, x, row : row + 2, :] = rrc[e + s, 0, 2 * j : 2 * j + 2, :]

    def mix(x):
        u = [raw[j, x] for j in range(3)]
        for i in range(2):
            q[i, x] = OLD[i][0] * u[0] + OLD[i][1] * u[1] + OLD[i][2] * u[2]

    def mix_potential(x):
        u = [raw[j, x + 1] for j in range(3)]
        w = [c * (c * c - 1.0) for c in u]
        for i, m in ((0, mu), (1, mu2)):
            cube = OLD[i][0] * w[0] + OLD[i][1] * w[1] + OLD[i][2] * w[2]
            m[x] = cube - around(q[i, x + 1], q[i, x], q[i, x + 2])

    def mix_force(x):
        k0[x + 4] = around(mu[x + 1], mu[x], mu[x + 2])
        k1[x + 2] = around(mu2[x + 1], mu2[x], mu2[x + 2])

    loop(20, mix)
    loop(18, mix_potential)

    def wide_halo(p, r, ys, yr, cr, ss, rs):
        ys[0, :, 0:4, :] = p[4:20, 20:24, :]
        ys[0, :, 4:6, :] = r[2:18, 22:24, :]
        ys[1, :, 0:4, :] = p[4:20, 8:12, :]
        ys[1, :, 4:6, :] = r[2:18, 8:10, :]
        copies = []
        for k, (dx, dy) in enumerate(DIRS):
            to = at(0, dx, dy)
            if dy == 0:
                rows = pl.ds(8, 16)
                own = pl.ds(16, 4) if dx > 0 else pl.ds(4, 4)
                copies.append(
                    send(p.at[own, rows], p.at[halo(4, dx, 4), rows], ss.at[k], rs.at[k], to)
                )
                own = pl.ds(16, 2) if dx > 0 else pl.ds(2, 2)
                copies.append(
                    send(r.at[own, rows], r.at[halo(2, dx, 2), rows], ss.at[8 + k], rs.at[8 + k], to)
                )
            elif dx == 0:
                s = (1 - dy) // 2
                copies.append(send(ys.at[s], yr.at[s], ss.at[k], rs.at[k], to))
            else:
                s = (1 - dy) // 2
                copies.append(send(ys.at[s, edge(3, dx)], cr.at[k - 4], ss.at[k], rs.at[k], to))
        return copies

    def place(copies, p, r, yr, cr):
        for copy in copies:
            copy.wait_recv()
        for s, low, near in ((0, 4, 6), (1, 24, 24)):
            p[4:20, low : low + 4, :] = yr[s, :, 0:4, :]
            r[2:18, near : near + 2, :] = yr[s, :, 4:6, :]
            p[1:4, low : low + 4, :] = cr[s, :, 0:4, :]
            r[1, near : near + 2, :] = cr[s, 2, 4:6, :]
            p[20:23, low : low + 4, :] = cr[2 + s, :, 0:4, :]
            r[18, near : near + 2, :] = cr[2 + s, 0, 4:6, :]

    def mix_force_stored(x):
        rows = pl.ds(8, 16)
        k0[x + 4, rows, :] = around(mu[x + 1], mu[x], mu[x + 2])[8:24]
        k1[x + 2, rows, :] = around(mu2[x + 1], mu2[x], mu2[x + 2])[8:24]

    loop(16, mix_force_stored)
    ks = wide_halo(k0, k1, ksy, kry, krc, k_s, k_r)

    @pl.when(n == 0)
    def _():
        start[6:22, 8:24, :] = g[0, 0]

    @pl.when(n > 0)
    def _():
        along.wait_recv()

    starts = []
    for k, (dx, dy) in enumerate(DIRS):
        if dy == 0:
            width = 6
        else:
            width = 5
        if dx == 0:
            xs = xd = pl.ds(6, 16)
        else:
            xs = pl.ds(22 - width, width) if dx > 0 else pl.ds(6, width)
            xd = pl.ds(6 - width, width) if dx > 0 else pl.ds(22, width)
        if dy == 0:
            ys = yd = pl.ds(8, 16)
        else:
            ys = pl.ds(16, 8) if dy > 0 else pl.ds(8, 8)
            yd = pl.ds(0, 8) if dy > 0 else pl.ds(24, 8)
        starts.append(
            send(start.at[xs, ys], start.at[xd, yd], s_s.at[k], s_r.at[k], at(0, dx, dy))
        )
    place(ks, k0, k1, kry, krc)
    for copy in starts:
        copy.wait_recv()

    potential(start, mu, 26)

    def first(x):
        f = around(mu[x + 1], mu[x], mu[x + 2])
        fs[x] = f
        u11[x] = start[x + 2] + HALF * f + k0[x]

    loop(24, first)
    potential(u11, mu, 22)

    def second(x):
        f = around(mu[x + 1], mu[x], mu[x + 2])
        f11[x] = f
        u12[x] = u11[x + 2] + HALF * f + k1[x]

    loop(20, second)
    potential(u12, mu, 18)

    def third(x):
        f2 = around(mu[x + 1], mu[x], mu[x + 2])[8:24]
        f0 = fs[x + 4, 8:24, :]
        f1 = f11[x + 2, 8:24, :]
        rows = pl.ds(8, 16)
        u21[x + 4, rows, :] = start[x + 6, 8:24, :] + DT * (W[0][0] * f0 + W[0][1] * f1 + W[0][2] * f2)
        bb[x + 2, rows, :] = OLD[1][0] * f0 + OLD[1][1] * f1 + OLD[1][2] * f2

    loop(16, third)
    us = wide_halo(u21, bb, usy, ury, urc, u_s, u_r)

    def restrict(read, count, rows):
        both = [(read(2 * i) + read(2 * i + 1)) * 0.25 for i in range(count)]
        flat = jnp.concatenate(both, axis=0)
        pair[0 : count * rows, :] = dot(flat, zavg[...])
        total = count * rows // 2
        return pair[pl.ds(0, total, stride=2), :] + pair[pl.ds(1, total, stride=2), :]

    def coarse_force(values):
        v = values.reshape(12, 16, 128)
        c = v[1:-1]
        m = c * (c * c - 1.0) - 0.25 * around3(v)
        co[...] = 0.25 * around3(m)
        return co[:, 4:12, :].reshape(64, 128)

    c0 = restrict(lambda x: start[x + 2], 12, 32)
    g0 = coarse_force(c0)
    co[...] = c0.reshape(12, 16, 128)[2:10]
    cb[0] = co[:, 4:12, :].reshape(64, 128)

    place(us, u21, bb, ury, urc)
    potential(u21, mu, 22)

    def fourth(x):
        f = around(mu[x + 1], mu[x], mu[x + 2])
        f21[x] = f
        u22[x] = u21[x + 2] + HALF * f + bb[x]

    loop(20, fourth)
    potential(u22, mu, 18)

    def fifth(x):
        f2 = around(mu[x + 1], mu[x], mu[x + 2])[8:24]
        f0 = fs[x + 4, 8:24, :]
        f1 = f21[x + 2, 8:24, :]
        j0[x] = DT * (W[0][0] * f0 + W[0][1] * f1 + W[0][2] * f2)
        j1[x] = DT * (W[1][0] * f0 + W[1][1] * f1 + W[1][2] * f2)

    loop(16, fifth)
    c1 = restrict(lambda x: u21[x], 12, 32)
    g1 = coarse_force(c1)
    co[...] = c1.reshape(12, 16, 128)[2:10]
    cb[1] = co[:, 4:12, :].reshape(64, 128)
    cb[2] = restrict(lambda x: u22[x + 2, 8:24, :], 8, 16)
    part0 = restrict(lambda x: j0[x], 8, 16)
    part1 = restrict(lambda x: j1[x], 8, 16)
    part0 = part0 + jnp.where(n == 0, cb[0], -HALF * g0)
    part1 = part1 - HALF * g1
    turned = jnp.transpose(jnp.concatenate([part0, part1], axis=0))
    xext[32:160, :] = turned
    xext[0:32, :] = turned[96:128]
    xext[160:192, :] = turned[0:32]

    block = a * 4 + b
    is_chain = jnp.logical_and(lax.rem(a, 2) == 0, b == lax.rem(n + a, 4))
    mine = jnp.where(is_chain, n + 8 * (a // 2), -1)

    for c in range(4):
        length = 72 - 16 * c

        @pl.when(n // 2 == c)
        def _():
            def each(p):
                src = xext.at[pl.ds(pl.multiple_of(8 * p + 8 * c, 8), length), :]
                dst = gath.at[n, block, pl.ds(8 * c, length), :]
                t = lax.rem(p, 8)
                x = 2 * (p // 8)

                @pl.when(p != mine)
                def _():
                    send(src, dst, g_s, g_r.at[n], (t, x, lax.rem(t + x, 4)))

                @pl.when(p == mine)
                def _():
                    pltpu.make_async_copy(src, dst, g_r.at[n]).start()

            loop(16, each, 1)

    lane = lax.broadcasted_iota(jnp.int32, (72, 128), 1)

    def chain_lap(ref, t, rows):
        x, y = t // 4, lax.rem(t, 4)
        c = ref[t, rows, :]
        o = ref[(1 - x) * 4 + y, rows, :]
        up = ref[x * 4 + lax.rem(y + 1, 4), rows, :]
        down = ref[x * 4 + lax.rem(y + 3, 4), rows, :]
        size = c.shape[0]
        l = lane[:size]
        s = jnp.where(l < 120, pltpu.roll(c, 120, 1), pltpu.roll(o, 120, 1))
        s = s + jnp.where(l >= 8, pltpu.roll(c, 8, 1), pltpu.roll(o, 8, 1))
        inner = l & 7
        s = s + jnp.where(inner < 7, pltpu.roll(c, 127, 1), pltpu.roll(up, 7, 1))
        s = s + jnp.where(inner > 0, pltpu.roll(c, 1, 1), pltpu.roll(down, 121, 1))
        s = s + pltpu.roll(c, 1, 0) + pltpu.roll(c, size - 1, 0)
        return c, 0.25 * (s - 6.0 * c)

    @pl.when(is_chain)
    def _():
        me = n + 8 * (a // 2)
        v0[...] = jnp.zeros_like(v0)

        def sweep(src, dst, rows, m, first):
            def one(t):
                c, l = chain_lap(src, t, rows)
                m0[t, rows, :] = c * (c * c - 1.0) - l

            def two(t):
                _, f = chain_lap(m0, t, rows)
                x, y = t // 4, lax.rem(t, 4)
                e, o = gath[m, 8 * x + y, rows, :], gath[m, 8 * x + 4 + y, rows, :]
                l = lane[: e.shape[0]]
                if first:
                    part = jnp.where(l < 64, e, pltpu.roll(o, 64, 1))
                else:
                    part = jnp.where(l < 64, pltpu.roll(e, 64, 1), o)
                dst[t, rows, :] = src[t, rows, :] + HALF * f + part

            loop(8, one, 1)
            loop(8, two, 1)

        for c in range(4):
            rows = pl.ds(8 * c, 72 - 16 * c)

            def turn(i):
                m = 2 * c + i
                whole = gath.at[m, :, rows, :]
                pltpu.make_async_copy(whole, whole, g_r.at[m]).wait()
                stage[m, :, 0] = v0[:, 32:40, :]
                sweep(v0, v1, rows, m, True)
                stage[m, :, 1] = v1[:, 32:40, :]
                sweep(v1, v0, rows, m, False)
                stage[m, :, 2] = v0[:, 32:40, :]

                def each(d):
                    x, y = d // 4, lax.rem(d, 4)
                    src = stage.at[m, (x // 2) * 4 + y]
                    dst = back.at[:, pl.ds(pl.multiple_of(8 * me, 8), 8), :]
                    own = jnp.logical_and(m == n, d == block)

                    @pl.when(jnp.logical_not(own))
                    def _():
                        send(src, dst, b_s, b_r, (m, x, y))

                    @pl.when(own)
                    def _():
                        pltpu.make_async_copy(src, dst, b_r).start()

                loop(16, each, 1)

            loop(2, turn, 1)

    pltpu.make_async_copy(back, back, b_r).wait()
    for j in range(3):
        half[...] = jnp.transpose(back[j])
        rows = pl.ds(pl.multiple_of(64 * lax.rem(a, 2), 64), 64)
        change = half[rows, :] - cb[j]
        if j == 0:
            change = jnp.where(n == 0, 0.0, change)
        fine = dot(dot(ydup[...], change), zdup[...])
        for i in range(8):
            add = fine[16 * i : 16 * i + 16]
            for x in (2 * i, 2 * i + 1):
                if j == 0:
                    node = start[x + 6, 8:24, :]
                elif j == 1:
                    node = u21[x + 4, 8:24, :]
                else:
                    node = u22[x + 2, 8:24, :]
                out[j, 0, x] = node + add

    @pl.when(n < 7)
    def _():
        along.wait_send()

    for copy in raws + ks + starts + us:
        copy.wait_send()
    for c in range(4):
        length = 72 - 16 * c

        @pl.when(n // 2 == c)
        def _():
            @pl.when(is_chain)
            def _():
                sent = gath.at[0, 0:15, pl.ds(8 * c, length), :]
                pltpu.make_async_copy(sent, sent, g_s).wait()

            @pl.when(jnp.logical_not(is_chain))
            def _():
                sent = gath.at[0, :, pl.ds(8 * c, length), :]
                pltpu.make_async_copy(sent, sent, g_s).wait()

    @pl.when(is_chain)
    def _():
        for m in range(8):
            count = stage.at[m]
            if m == 0:
                count = stage.at[0, 0:7]
            pltpu.make_async_copy(count, count, b_s).wait()
        for m in range(8):
            pltpu.make_async_copy(stage.at[m], stage.at[m], b_s).wait()


def local(guess):
    zavg = np.zeros((256, 128), np.float32)
    zavg[np.arange(256), np.arange(256) // 2] = 0.5
    zdup = np.zeros((128, 256), np.float32)
    zdup[np.arange(256) // 2, np.arange(256)] = 1.0
    ydup = np.zeros((128, 64), np.float32)
    r = np.arange(128)
    ydup[r, (r // 16) * 8 + (r % 16) // 2] = 1.0
    vm = lambda *s: pltpu.VMEM(s, F32)
    dma = lambda *s: pltpu.SemaphoreType.DMA(s)
    vspec = pl.BlockSpec(memory_space=pltpu.VMEM)
    return pl.pallas_call(
        kernel,
        out_shape=jax.ShapeDtypeStruct(guess.shape, F32),
        in_specs=[vspec] * 4,
        out_specs=vspec,
        scratch_shapes=[
            vm(3, 20, 32, 256), vm(2, 16, 8, 256), vm(2, 16, 8, 256), vm(4, 1, 8, 256),
            vm(2, 20, 32, 256), vm(28, 32, 256), vm(28, 32, 256),
            vm(28, 32, 256), vm(24, 32, 256), vm(20, 32, 256),
            vm(2, 16, 8, 256), vm(2, 16, 8, 256), vm(4, 3, 8, 256),
            vm(24, 32, 256), vm(20, 32, 256), vm(24, 32, 256), vm(20, 32, 256),
            vm(2, 16, 8, 256), vm(2, 16, 8, 256), vm(4, 3, 8, 256), vm(20, 32, 256),
            vm(24, 32, 256), vm(20, 32, 256), vm(20, 32, 256), vm(16, 16, 256), vm(16, 16, 256),
            vm(384, 128), vm(8, 16, 128), vm(3, 64, 128), vm(192, 128),
            vm(8, 16, 72, 128), vm(8, 72, 128), vm(8, 72, 128), vm(8, 72, 128),
            vm(8, 8, 3, 8, 128), vm(3, 128, 128), vm(128, 128),
            pltpu.SemaphoreType.DMA, pltpu.SemaphoreType.DMA,
            dma(8), dma(8), dma(10), dma(10), dma(8), dma(8), dma(10), dma(10),
            pltpu.SemaphoreType.DMA, dma(8), pltpu.SemaphoreType.DMA, pltpu.SemaphoreType.DMA,
        ],
        compiler_params=pltpu.CompilerParams(
            collective_id=0, has_side_effects=True, vmem_limit_bytes=48 * 1024 * 1024
        ),
    )(guess, jnp.asarray(zavg), jnp.asarray(zdup), jnp.asarray(ydup))


def solution(mesh):
    spec = P(None, "tm", "gx", "gy", None)
    return jax.shard_map(local, mesh=mesh, in_specs=(spec,), out_specs=spec, check_vma=False)
```

```python
import jax
import jax.numpy as jnp
from jax import lax
from jax.experimental import pallas as pl
from jax.experimental.pallas import tpu as pltpu
from jax.sharding import PartitionSpec as P

DT = 0.01
HALF = 0.005
W = ((5.0 / 24.0, 1.0 / 3.0, -1.0 / 24.0), (-1.0 / 24.0, 1.0 / 3.0, 5.0 / 24.0))
OLD = (
    (DT * (W[0][0] - 0.5), DT * W[0][1], DT * W[0][2]),
    (DT * W[1][0], DT * (W[1][1] - 0.5), DT * W[1][2]),
)
MESH = pl.DeviceIdType.MESH
DIRS = ((1, 0), (-1, 0), (0, 1), (0, -1), (1, 1), (1, -1), (-1, 1), (-1, -1))
F32 = jnp.float32
HIGH = lax.Precision.HIGHEST


def dot(a, b):
    return jnp.dot(a, b, precision=HIGH, preferred_element_type=F32)


def around(c, low, high):
    rows, z = c.shape
    s = (low + high) + (pltpu.roll(c, 1, 0) + pltpu.roll(c, rows - 1, 0))
    s = s + (pltpu.roll(c, 1, 1) + pltpu.roll(c, z - 1, 1))
    return s - 6.0 * c


def around3(v):
    c = v[1:-1]
    rows, z = c.shape[1:]
    s = v[:-2] + v[2:] + pltpu.roll(c, 1, 1) + pltpu.roll(c, rows - 1, 1)
    s = s + pltpu.roll(c, 1, 2) + pltpu.roll(c, z - 1, 2)
    return s - 6.0 * c


def loop(count, body, unroll=2):
    def step(i, carry):
        body(i)
        return carry

    lax.fori_loop(0, count, step, 0, unroll=unroll)


def potential(src, mu, count):
    def body(x):
        c = src[x + 1]
        mu[x] = c * (c * c - 1.0) - around(c, src[x], src[x + 2])

    loop(count, body)


def edge(h, d):
    return pl.ds(16 - h, h) if d > 0 else pl.ds(0, h)


def halo(h, d, at):
    return pl.ds(at - h, h) if d > 0 else pl.ds(at + 16, h)


def kernel(
    g, out,
    zavg, zdup, ydup, raw, rsy, rry, rrc, q, mu, mu2,
    start, k0, k1, ksy, kry, krc,
    u11, u12, u21, bb, usy, ury, urc, u22,
    fs, f11, f21, j0, j1,
    pair, co, cb, xext, gath, v0, v1, m0, stage, back, half,
    in_s, st_s, st_r, raw_s, raw_r, k_s, k_r, s_s, s_r, u_s, u_r, g_s, g_r, b_s, b_r,
):
    n, a, b = lax.axis_index("tm"), lax.axis_index("gx"), lax.axis_index("gy")

    def at(dt, dx, dy):
        return (lax.rem(n + dt + 8, 8), lax.rem(a + dx + 4, 4), lax.rem(b + dy + 4, 4))

    barrier = pltpu.get_barrier_semaphore()
    for dx, dy in DIRS:
        pl.semaphore_signal(barrier, inc=1, device_id=at(0, dx, dy), device_id_type=MESH)
    for dt in range(1, 8):
        pl.semaphore_signal(barrier, inc=1, device_id=at(dt, 0, 0), device_id_type=MESH)

    block16 = (pl.ds(2, 16), pl.ds(8, 16))
    loads = [pltpu.make_async_copy(g.at[j, 0], raw.at[j, *block16], in_s.at[j]) for j in range(3)]
    for load in loads:
        load.start()

    def iota(shape, d):
        return lax.broadcasted_iota(jnp.int32, shape, d)

    zavg[...] = jnp.where(iota((256, 128), 0) // 2 == iota((256, 128), 1), 0.5, 0.0)
    zdup[...] = jnp.where(iota((128, 256), 0) == iota((128, 256), 1) // 2, 1.0, 0.0)
    r, k = iota((128, 64), 0), iota((128, 64), 1)
    ydup[...] = jnp.where(k == (r // 16) * 8 + lax.rem(r, 16) // 2, 1.0, 0.0)
    for load in loads:
        load.wait()
    for j in range(3):
        rsy[0, :, 2 * j : 2 * j + 2, :] = raw[j, 2:18, 22:24, :]
        rsy[1, :, 2 * j : 2 * j + 2, :] = raw[j, 2:18, 8:10, :]
    pl.semaphore_wait(barrier, 15)

    def send(src, dst, ss, rs, to):
        copy = pltpu.make_async_remote_copy(
            src_ref=src, dst_ref=dst, send_sem=ss, recv_sem=rs, device_id=to, device_id_type=MESH
        )
        copy.start()
        return copy

    mid = start.at[pl.ds(6, 16), pl.ds(8, 16), :]
    along = pltpu.make_async_remote_copy(
        src_ref=raw.at[2, *block16], dst_ref=mid, send_sem=st_s, recv_sem=st_r,
        device_id=at(1, 0, 0), device_id_type=MESH,
    )

    @pl.when(n < 7)
    def _():
        along.start()

    raws = []
    for k, (dx, dy) in enumerate(DIRS):
        if dy == 0:
            src = raw.at[:, pl.ds(16, 2) if dx > 0 else pl.ds(2, 2), pl.ds(8, 16), :]
            dst = raw.at[:, halo(2, dx, 2), pl.ds(8, 16), :]
        elif dx == 0:
            src, dst = rsy.at[(1 - dy) // 2], rry.at[(1 - dy) // 2]
        else:
            src, dst = rsy.at[(1 - dy) // 2, edge(1, dx)], rrc.at[k - 4]
        raws.append(send(src, dst, raw_s.at[k], raw_r.at[k], at(0, dx, dy)))
    @pl.when(n == 0)
    def _():
        start[6:22, 8:24, :] = raw[0, 2:18, 8:24, :]

    @pl.when(n > 0)
    def _():
        along.wait_recv()

    starts = []
    for k, (dx, dy) in enumerate(DIRS):
        if dy == 0:
            width = 6
        else:
            width = 5
        if dx == 0:
            xs = xd = pl.ds(6, 16)
        else:
            xs = pl.ds(22 - width, width) if dx > 0 else pl.ds(6, width)
            xd = pl.ds(6 - width, width) if dx > 0 else pl.ds(22, width)
        if dy == 0:
            ys = yd = pl.ds(8, 16)
        else:
            ys = pl.ds(16, 8) if dy > 0 else pl.ds(8, 8)
            yd = pl.ds(0, 8) if dy > 0 else pl.ds(24, 8)
        starts.append(
            send(start.at[xs, ys], start.at[xd, yd], s_s.at[k], s_r.at[k], at(0, dx, dy))
        )
    for copy in raws:
        copy.wait_recv()
    for s, row in ((0, 6), (1, 24)):
        for j in range(3):
            raw[j, 2:18, row : row + 2, :] = rry[s, :, 2 * j : 2 * j + 2, :]
            for e, x in ((0, 1), (2, 18)):
                raw[j, x, row : row + 2, :] = rrc[e + s, 0, 2 * j : 2 * j + 2, :]

    def mix(x):
        u = [raw[j, x] for j in range(3)]
        for i in range(2):
            q[i, x] = OLD[i][0] * u[0] + OLD[i][1] * u[1] + OLD[i][2] * u[2]

    def mix_potential(x):
        u = [raw[j, x + 1] for j in range(3)]
        w = [c * (c * c - 1.0) for c in u]
        for i, m in ((0, mu), (1, mu2)):
            cube = OLD[i][0] * w[0] + OLD[i][1] * w[1] + OLD[i][2] * w[2]
            m[x] = cube - around(q[i, x + 1], q[i, x], q[i, x + 2])

    loop(20, mix)
    loop(18, mix_potential)

    def wide_halo(p, r, ys, yr, cr, ss, rs):
        ys[0, :, 0:4, :] = p[4:20, 20:24, :]
        ys[0, :, 4:6, :] = r[2:18, 22:24, :]
        ys[1, :, 0:4, :] = p[4:20, 8:12, :]
        ys[1, :, 4:6, :] = r[2:18, 8:10, :]
        copies = []
        for k, (dx, dy) in enumerate(DIRS):
            to = at(0, dx, dy)
            if dy == 0:
                rows = pl.ds(8, 16)
                own = pl.ds(16, 4) if dx > 0 else pl.ds(4, 4)
                copies.append(
                    send(p.at[own, rows], p.at[halo(4, dx, 4), rows], ss.at[k], rs.at[k], to)
                )
                own = pl.ds(16, 2) if dx > 0 else pl.ds(2, 2)
                copies.append(
                    send(r.at[own, rows], r.at[halo(2, dx, 2), rows], ss.at[8 + k], rs.at[8 + k], to)
                )
            elif dx == 0:
                s = (1 - dy) // 2
                copies.append(send(ys.at[s], yr.at[s], ss.at[k], rs.at[k], to))
            else:
                s = (1 - dy) // 2
                copies.append(send(ys.at[s, edge(3, dx)], cr.at[k - 4], ss.at[k], rs.at[k], to))
        return copies

    def place(copies, p, r, yr, cr):
        for copy in copies:
            copy.wait_recv()
        for s, low, near in ((0, 4, 6), (1, 24, 24)):
            p[4:20, low : low + 4, :] = yr[s, :, 0:4, :]
            r[2:18, near : near + 2, :] = yr[s, :, 4:6, :]
            p[1:4, low : low + 4, :] = cr[s, :, 0:4, :]
            r[1, near : near + 2, :] = cr[s, 2, 4:6, :]
            p[20:23, low : low + 4, :] = cr[2 + s, :, 0:4, :]
            r[18, near : near + 2, :] = cr[2 + s, 0, 4:6, :]

    def mix_force_stored(x):
        rows = pl.ds(8, 16)
        k0[x + 4, rows, :] = around(mu[x + 1], mu[x], mu[x + 2])[8:24]
        k1[x + 2, rows, :] = around(mu2[x + 1], mu2[x], mu2[x + 2])[8:24]

    loop(16, mix_force_stored)
    ks = wide_halo(k0, k1, ksy, kry, krc, k_s, k_r)

    place(ks, k0, k1, kry, krc)
    for copy in starts:
        copy.wait_recv()

    potential(start, mu, 26)

    def first(x):
        f = around(mu[x + 1], mu[x], mu[x + 2])
        fs[x] = f
        u11[x] = start[x + 2] + HALF * f + k0[x]

    loop(24, first)
    potential(u11, mu, 22)

    def second(x):
        f = around(mu[x + 1], mu[x], mu[x + 2])
        f11[x] = f
        u12[x] = u11[x + 2] + HALF * f + k1[x]

    loop(20, second)
    potential(u12, mu, 18)

    def third(x):
        f2 = around(mu[x + 1], mu[x], mu[x + 2])[8:24]
        f0 = fs[x + 4, 8:24, :]
        f1 = f11[x + 2, 8:24, :]
        rows = pl.ds(8, 16)
        u21[x + 4, rows, :] = start[x + 6, 8:24, :] + DT * (W[0][0] * f0 + W[0][1] * f1 + W[0][2] * f2)
        bb[x + 2, rows, :] = OLD[1][0] * f0 + OLD[1][1] * f1 + OLD[1][2] * f2

    loop(16, third)
    us = wide_halo(u21, bb, usy, ury, urc, u_s, u_r)

    def restrict(read, count, rows):
        both = [(read(2 * i) + read(2 * i + 1)) * 0.25 for i in range(count)]
        flat = jnp.concatenate(both, axis=0)
        pair[0 : count * rows, :] = dot(flat, zavg[...])
        total = count * rows // 2
        return pair[pl.ds(0, total, stride=2), :] + pair[pl.ds(1, total, stride=2), :]

    def coarse_force(values):
        v = values.reshape(12, 16, 128)
        c = v[1:-1]
        m = c * (c * c - 1.0) - 0.25 * around3(v)
        co[...] = 0.25 * around3(m)
        return co[:, 4:12, :].reshape(64, 128)

    c0 = restrict(lambda x: start[x + 2], 12, 32)
    g0 = coarse_force(c0)
    co[...] = c0.reshape(12, 16, 128)[2:10]
    cb[0] = co[:, 4:12, :].reshape(64, 128)

    place(us, u21, bb, ury, urc)
    potential(u21, mu, 22)

    def fourth(x):
        f = around(mu[x + 1], mu[x], mu[x + 2])
        f21[x] = f
        u22[x] = u21[x + 2] + HALF * f + bb[x]

    loop(20, fourth)
    potential(u22, mu, 18)

    def fifth(x):
        f2 = around(mu[x + 1], mu[x], mu[x + 2])[8:24]
        f0 = fs[x + 4, 8:24, :]
        f1 = f21[x + 2, 8:24, :]
        j0[x] = DT * (W[0][0] * f0 + W[0][1] * f1 + W[0][2] * f2)
        j1[x] = DT * (W[1][0] * f0 + W[1][1] * f1 + W[1][2] * f2)

    loop(16, fifth)
    c1 = restrict(lambda x: u21[x], 12, 32)
    g1 = coarse_force(c1)
    co[...] = c1.reshape(12, 16, 128)[2:10]
    cb[1] = co[:, 4:12, :].reshape(64, 128)
    cb[2] = restrict(lambda x: u22[x + 2, 8:24, :], 8, 16)
    part0 = restrict(lambda x: j0[x], 8, 16)
    part1 = restrict(lambda x: j1[x], 8, 16)
    part0 = part0 + jnp.where(n == 0, cb[0], -HALF * g0)
    part1 = part1 - HALF * g1
    turned = jnp.transpose(jnp.concatenate([part0, part1], axis=0))
    xext[32:160, :] = turned
    xext[0:32, :] = turned[96:128]
    xext[160:192, :] = turned[0:32]

    block = a * 4 + b
    is_chain = jnp.logical_and(lax.rem(a, 2) == 0, b == lax.rem(n + a, 4))
    mine = jnp.where(is_chain, n + 8 * (a // 2), -1)

    for c in range(4):
        length = 72 - 16 * c

        @pl.when(n // 2 == c)
        def _():
            def each(p):
                src = xext.at[pl.ds(pl.multiple_of(8 * p + 8 * c, 8), length), :]
                dst = gath.at[n, block, pl.ds(8 * c, length), :]
                t = lax.rem(p, 8)
                x = 2 * (p // 8)

                @pl.when(p != mine)
                def _():
                    send(src, dst, g_s, g_r.at[n], (t, x, lax.rem(t + x, 4)))

                @pl.when(p == mine)
                def _():
                    pltpu.make_async_copy(src, dst, g_r.at[n]).start()

            loop(16, each, 1)

    lane = lax.broadcasted_iota(jnp.int32, (8, 128), 1)
    inner = lane & 7

    def chain_lap(ref, lo, hi, put):
        for r in range(lo, hi, 8):
            c = [ref[t, r : r + 8, :] for t in range(8)]
            turn = lambda by: [pltpu.roll(v, by % 128, 1) for v in c]
            xp, xm, yp, ym, yu, yd = (turn(by) for by in (-8, 8, -1, 1, 7, -7))
            for t in range(8):
                o, up, down = (t + 4) % 8, t // 4 * 4 + (t + 1) % 4, t // 4 * 4 + (t + 3) % 4
                s = jnp.where(lane < 120, xp[t], xp[o]) + jnp.where(lane >= 8, xm[t], xm[o])
                s = s + (jnp.where(inner < 7, yp[t], yu[up]) + jnp.where(inner > 0, ym[t], yd[down]))
                s = s + (ref[t, r + 1 : r + 9, :] + ref[t, r - 1 : r + 7, :])
                put(t, r, c[t], 0.25 * (s - 6.0 * c[t]))

    @pl.when(is_chain)
    def _():
        me = n + 8 * (a // 2)
        v0[...] = jnp.zeros_like(v0)

        def sweep(src, dst, c, m, first):
            lo, hi = 8 + 8 * c, 80 - 8 * c

            def one(t, r, u, l):
                m0[t, r : r + 8, :] = u * (u * u - 1.0) - l

            def two(t, r, u, f):
                x, y = t // 4, t % 4
                rows = pl.ds(r - 8, 8)
                e, o = gath[m, 8 * x + y, rows, :], gath[m, 8 * x + 4 + y, rows, :]
                if first:
                    part = jnp.where(lane < 64, e, pltpu.roll(o, 64, 1))
                else:
                    part = jnp.where(lane < 64, pltpu.roll(e, 64, 1), o)
                dst[t, r : r + 8, :] = src[t, r : r + 8, :] + HALF * f + part

            chain_lap(src, lo, hi, one)
            chain_lap(m0, lo, hi, two)

        for c in range(4):
            rows = pl.ds(8 * c, 72 - 16 * c)

            def turn(i):
                m = 2 * c + i
                whole = gath.at[m, :, rows, :]
                pltpu.make_async_copy(whole, whole, g_r.at[m]).wait()
                stage[m, :, 0] = v0[:, 40:48, :]
                sweep(v0, v1, c, m, True)
                stage[m, :, 1] = v1[:, 40:48, :]
                sweep(v1, v0, c, m, False)
                stage[m, :, 2] = v0[:, 40:48, :]

                def each(d):
                    x, y = d // 4, lax.rem(d, 4)
                    src = stage.at[m, (x // 2) * 4 + y]
                    dst = back.at[:, pl.ds(pl.multiple_of(8 * me, 8), 8), :]
                    own = jnp.logical_and(m == n, d == block)

                    @pl.when(jnp.logical_not(own))
                    def _():
                        send(src, dst, b_s, b_r, (m, x, y))

                    @pl.when(own)
                    def _():
                        pltpu.make_async_copy(src, dst, b_r).start()

                loop(16, each, 1)

            loop(2, turn, 1)

    pltpu.make_async_copy(back, back, b_r).wait()
    for j in range(3):
        half[...] = jnp.transpose(back[j])
        rows = pl.ds(pl.multiple_of(64 * lax.rem(a, 2), 64), 64)
        change = half[rows, :] - cb[j]
        if j == 0:
            change = jnp.where(n == 0, 0.0, change)
        fine = dot(dot(ydup[...], change), zdup[...])
        for i in range(8):
            add = fine[16 * i : 16 * i + 16]
            for x in (2 * i, 2 * i + 1):
                if j == 0:
                    node = start[x + 6, 8:24, :]
                elif j == 1:
                    node = u21[x + 4, 8:24, :]
                else:
                    node = u22[x + 2, 8:24, :]
                out[j, 0, x] = node + add

    @pl.when(n < 7)
    def _():
        along.wait_send()

    for copy in raws + ks + starts + us:
        copy.wait_send()
    for c in range(4):
        length = 72 - 16 * c

        @pl.when(n // 2 == c)
        def _():
            @pl.when(is_chain)
            def _():
                sent = gath.at[0, 0:15, pl.ds(8 * c, length), :]
                pltpu.make_async_copy(sent, sent, g_s).wait()

            @pl.when(jnp.logical_not(is_chain))
            def _():
                sent = gath.at[0, :, pl.ds(8 * c, length), :]
                pltpu.make_async_copy(sent, sent, g_s).wait()

    @pl.when(is_chain)
    def _():
        for m in range(8):
            count = stage.at[m]
            if m == 0:
                count = stage.at[0, 0:7]
            pltpu.make_async_copy(count, count, b_s).wait()
        for m in range(8):
            pltpu.make_async_copy(stage.at[m], stage.at[m], b_s).wait()


def local(guess):
    vm = lambda *s: pltpu.VMEM(s, F32)
    dma = lambda *s: pltpu.SemaphoreType.DMA(s)
    vspec = pl.BlockSpec(memory_space=pltpu.VMEM)
    return pl.pallas_call(
        kernel,
        out_shape=jax.ShapeDtypeStruct(guess.shape, F32),
        in_specs=[pl.BlockSpec(memory_space=pl.ANY)],
        out_specs=vspec,
        scratch_shapes=[
            vm(256, 128), vm(128, 256), vm(128, 64),
            vm(3, 20, 32, 256), vm(2, 16, 8, 256), vm(2, 16, 8, 256), vm(4, 1, 8, 256),
            vm(2, 20, 32, 256), vm(28, 32, 256), vm(28, 32, 256),
            vm(28, 32, 256), vm(24, 32, 256), vm(20, 32, 256),
            vm(2, 16, 8, 256), vm(2, 16, 8, 256), vm(4, 3, 8, 256),
            vm(24, 32, 256), vm(20, 32, 256), vm(24, 32, 256), vm(20, 32, 256),
            vm(2, 16, 8, 256), vm(2, 16, 8, 256), vm(4, 3, 8, 256), vm(20, 32, 256),
            vm(24, 32, 256), vm(20, 32, 256), vm(20, 32, 256), vm(16, 16, 256), vm(16, 16, 256),
            vm(384, 128), vm(8, 16, 128), vm(3, 64, 128), vm(192, 128),
            vm(8, 16, 72, 128), vm(8, 88, 128), vm(8, 88, 128), vm(8, 88, 128),
            vm(8, 8, 3, 8, 128), vm(3, 128, 128), vm(128, 128),
            dma(3), pltpu.SemaphoreType.DMA, pltpu.SemaphoreType.DMA,
            dma(8), dma(8), dma(10), dma(10), dma(8), dma(8), dma(10), dma(10),
            pltpu.SemaphoreType.DMA, dma(8), pltpu.SemaphoreType.DMA, pltpu.SemaphoreType.DMA,
        ],
        compiler_params=pltpu.CompilerParams(
            collective_id=0, has_side_effects=True, vmem_limit_bytes=48 * 1024 * 1024
        ),
    )(guess)


def solution(mesh):
    spec = P(None, "tm", "gx", "gy", None)
    return jax.shard_map(local, mesh=mesh, in_specs=(spec,), out_specs=spec, check_vma=False)
```

```python
import jax
import jax.numpy as jnp
from jax import lax
from jax.experimental import pallas as pl
from jax.experimental.pallas import tpu as pltpu
from jax.sharding import PartitionSpec as P

DT = 0.01
HALF = 0.005
W = ((5.0 / 24.0, 1.0 / 3.0, -1.0 / 24.0), (-1.0 / 24.0, 1.0 / 3.0, 5.0 / 24.0))
OLD = (
    (DT * (W[0][0] - 0.5), DT * W[0][1], DT * W[0][2]),
    (DT * W[1][0], DT * (W[1][1] - 0.5), DT * W[1][2]),
)
MESH = pl.DeviceIdType.MESH
DIRS = ((1, 0), (-1, 0), (0, 1), (0, -1), (1, 1), (1, -1), (-1, 1), (-1, -1))
F32 = jnp.float32
HIGH = lax.Precision.HIGHEST


def dot(a, b):
    return jnp.dot(a, b, precision=HIGH, preferred_element_type=F32)


def around(c, low, high):
    rows, z = c.shape
    s = (low + high) + (pltpu.roll(c, 1, 0) + pltpu.roll(c, rows - 1, 0))
    s = s + (pltpu.roll(c, 1, 1) + pltpu.roll(c, z - 1, 1))
    return s - 6.0 * c


def around3(v):
    c = v[1:-1]
    rows, z = c.shape[1:]
    s = v[:-2] + v[2:] + pltpu.roll(c, 1, 1) + pltpu.roll(c, rows - 1, 1)
    s = s + pltpu.roll(c, 1, 2) + pltpu.roll(c, z - 1, 2)
    return s - 6.0 * c


def loop(count, body, group=1):
    def step(i, carry):
        base = jnp.minimum(group * i, count - group)
        for k in range(group):
            body(base + k)
        return carry

    lax.fori_loop(0, -(-count // group), step, 0)


def potential(src, mu, count, group):
    def body(x):
        c = src[x + 1]
        mu[x] = c * (c * c - 1.0) - around(c, src[x], src[x + 2])

    loop(count, body, group)


def crop(v):
    return pltpu.roll(v, 28, 0)[0:24]


def edge(h, d):
    return pl.ds(16 - h, h) if d > 0 else pl.ds(0, h)


def halo(h, d, at):
    return pl.ds(at - h, h) if d > 0 else pl.ds(at + 16, h)


def kernel(
    g, out,
    zavg, zdup, ydup, raw, rsy, rry, rrc, q, w, mu, mu2,
    start, k0, k1, ksx, krx, ksy, kry, krc,
    u11, u12, u21, bb, usx, urx, usy, ury, urc, u22,
    fs, f11, f21, j0, j1, wide,
    pair, co, cb, xext, gath, v0, v1, m0, seam, stage, back, half,
    in_s, st_s, st_r, raw_s, raw_r, k_s, k_r, s_s, s_r, u_s, u_r, g_s, g_r, x_s, x_r, b_s, b_r,
):
    n, a, b = lax.axis_index("tm"), lax.axis_index("gx"), lax.axis_index("gy")

    def at(dt, dx, dy):
        return (lax.rem(n + dt + 8, 8), lax.rem(a + dx + 4, 4), lax.rem(b + dy + 4, 4))

    barrier = pltpu.get_barrier_semaphore()
    for dx, dy in DIRS:
        pl.semaphore_signal(barrier, inc=1, device_id=at(0, dx, dy), device_id_type=MESH)
    for dt in range(1, 8):
        pl.semaphore_signal(barrier, inc=1, device_id=at(dt, 0, 0), device_id_type=MESH)

    block16 = (pl.ds(2, 16), pl.ds(8, 16))
    loads = [pltpu.make_async_copy(g.at[j, 0], raw.at[j, *block16], in_s.at[j]) for j in range(3)]
    for load in loads:
        load.start()

    def iota(shape, d):
        return lax.broadcasted_iota(jnp.int32, shape, d)

    zavg[...] = jnp.where(iota((256, 128), 0) // 2 == iota((256, 128), 1), 0.5, 0.0)
    zdup[...] = jnp.where(iota((128, 256), 0) == iota((128, 256), 1) // 2, 1.0, 0.0)
    r, k = iota((128, 64), 0), iota((128, 64), 1)
    ydup[...] = jnp.where(k == (r // 16) * 8 + lax.rem(r, 16) // 2, 1.0, 0.0)
    for load in loads:
        load.wait()
    for j in range(3):
        rsy[0, :, 2 * j : 2 * j + 2, :] = raw[j, 2:18, 22:24, :]
        rsy[1, :, 2 * j : 2 * j + 2, :] = raw[j, 2:18, 8:10, :]
    pl.semaphore_wait(barrier, 15)

    def send(src, dst, ss, rs, to):
        copy = pltpu.make_async_remote_copy(
            src_ref=src, dst_ref=dst, send_sem=ss, recv_sem=rs, device_id=to, device_id_type=MESH
        )
        copy.start()
        return copy

    mid = start.at[pl.ds(6, 16), pl.ds(8, 16), :]
    along = pltpu.make_async_remote_copy(
        src_ref=raw.at[2, *block16], dst_ref=mid, send_sem=st_s, recv_sem=st_r,
        device_id=at(1, 0, 0), device_id_type=MESH,
    )

    @pl.when(n < 7)
    def _():
        along.start()

    raws = []
    for k, (dx, dy) in enumerate(DIRS):
        if dy == 0:
            src = raw.at[:, pl.ds(16, 2) if dx > 0 else pl.ds(2, 2), pl.ds(8, 16), :]
            dst = raw.at[:, halo(2, dx, 2), pl.ds(8, 16), :]
        elif dx == 0:
            src, dst = rsy.at[(1 - dy) // 2], rry.at[(1 - dy) // 2]
        else:
            src, dst = rsy.at[(1 - dy) // 2, edge(1, dx)], rrc.at[k - 4]
        raws.append(send(src, dst, raw_s.at[k], raw_r.at[k], at(0, dx, dy)))
    @pl.when(n == 0)
    def _():
        start[6:22, 8:24, :] = raw[0, 2:18, 8:24, :]

    @pl.when(n > 0)
    def _():
        along.wait_recv()

    starts = []
    for k, (dx, dy) in enumerate(DIRS):
        if dy == 0:
            width = 6
        else:
            width = 5
        if dx == 0:
            xs = xd = pl.ds(6, 16)
        else:
            xs = pl.ds(22 - width, width) if dx > 0 else pl.ds(6, width)
            xd = pl.ds(6 - width, width) if dx > 0 else pl.ds(22, width)
        if dy == 0:
            ys = yd = pl.ds(8, 16)
        else:
            ys = pl.ds(16, 8) if dy > 0 else pl.ds(8, 8)
            yd = pl.ds(0, 8) if dy > 0 else pl.ds(24, 8)
        starts.append(
            send(start.at[xs, ys], start.at[xd, yd], s_s.at[k], s_r.at[k], at(0, dx, dy))
        )
    for copy in raws:
        copy.wait_recv()
    for s, row in ((0, 6), (1, 24)):
        for j in range(3):
            raw[j, 2:18, row : row + 2, :] = rry[s, :, 2 * j : 2 * j + 2, :]
            for e, x in ((0, 1), (2, 18)):
                raw[j, x, row : row + 2, :] = rrc[e + s, 0, 2 * j : 2 * j + 2, :]

    def mix(x):
        u = [raw[j, x] for j in range(3)]
        c = [v * (v * v - 1.0) for v in u]
        for i in range(2):
            q[i, x] = crop(OLD[i][0] * u[0] + OLD[i][1] * u[1] + OLD[i][2] * u[2])
            w[i, x] = crop(OLD[i][0] * c[0] + OLD[i][1] * c[1] + OLD[i][2] * c[2])

    def mix_potential(x):
        for i, m in ((0, mu), (1, mu2)):
            m[x] = w[i, x + 1] - around(q[i, x + 1], q[i, x], q[i, x + 2])

    def mix_force(x):
        k0[x + 4, 4:20, :] = around(mu[x + 1], mu[x], mu[x + 2])[4:20]
        k1[x + 2, 4:20, :] = around(mu2[x + 1], mu2[x], mu2[x + 2])[4:20]

    loop(20, mix, 5)
    loop(18, mix_potential, 6)
    loop(16, mix_force, 4)

    def wide_halo(p, r, xs, xr, ys, yr, cr, ss, rs):
        ys[0, :, 0:4, :] = p[4:20, 16:20, :]
        ys[0, :, 4:6, :] = r[2:18, 18:20, :]
        ys[1, :, 0:4, :] = p[4:20, 4:8, :]
        ys[1, :, 4:6, :] = r[2:18, 4:6, :]
        xs[0, 0:4] = p[16:20, 4:20, :]
        xs[0, 4:6] = r[16:18, 4:20, :]
        xs[1, 0:4] = p[4:8, 4:20, :]
        xs[1, 4:6] = r[2:4, 4:20, :]
        copies = []
        for k, (dx, dy) in enumerate(DIRS):
            s = (1 - dy) // 2
            if dy == 0:
                src, dst = xs.at[(1 - dx) // 2], xr.at[(1 - dx) // 2]
            elif dx == 0:
                src, dst = ys.at[s], yr.at[s]
            else:
                src, dst = ys.at[s, edge(3, dx)], cr.at[k - 4]
            copies.append(send(src, dst, ss.at[k], rs.at[k], at(0, dx, dy)))
        return copies

    def place(copies, p, r, xr, yr, cr):
        for copy in copies:
            copy.wait_recv()
        p[0:4, 4:20, :] = xr[0, 0:4]
        r[0:2, 4:20, :] = xr[0, 4:6]
        p[20:24, 4:20, :] = xr[1, 0:4]
        r[18:20, 4:20, :] = xr[1, 4:6]
        for s, low, near in ((0, 0, 2), (1, 20, 20)):
            p[4:20, low : low + 4, :] = yr[s, :, 0:4, :]
            r[2:18, near : near + 2, :] = yr[s, :, 4:6, :]
            p[1:4, low : low + 4, :] = cr[s, :, 0:4, :]
            r[1, near : near + 2, :] = cr[s, 2, 4:6, :]
            p[20:23, low : low + 4, :] = cr[2 + s, :, 0:4, :]
            r[18, near : near + 2, :] = cr[2 + s, 0, 4:6, :]

    ks = wide_halo(k0, k1, ksx, krx, ksy, kry, krc, k_s, k_r)

    for copy in starts:
        copy.wait_recv()
    potential(start, wide, 26, 9)
    place(ks, k0, k1, krx, kry, krc)

    def first(x):
        f = around(wide[x + 1], wide[x], wide[x + 2])
        fs[x] = crop(f)
        u11[x] = crop(start[x + 2] + HALF * f) + k0[x]

    loop(24, first, 8)
    potential(u11, mu, 22, 8)

    def second(x):
        f = around(mu[x + 1], mu[x], mu[x + 2])
        f11[x] = f
        u12[x] = u11[x + 2] + HALF * f + k1[x]

    loop(20, second, 10)
    potential(u12, mu, 18, 9)

    def third(x):
        f2 = around(mu[x + 1], mu[x], mu[x + 2])
        f0, f1 = fs[x + 4], f11[x + 2]
        new = crop(start[x + 6]) + DT * (W[0][0] * f0 + W[0][1] * f1 + W[0][2] * f2)
        u21[x + 4, 4:20, :] = new[4:20]
        bb[x + 2, 4:20, :] = (OLD[1][0] * f0 + OLD[1][1] * f1 + OLD[1][2] * f2)[4:20]

    loop(16, third, 8)
    us = wide_halo(u21, bb, usx, urx, usy, ury, urc, u_s, u_r)

    def average(layers, rows):
        both = [(layers[2 * i] + layers[2 * i + 1]) * 0.25 for i in range(len(layers) // 2)]
        pair[0 : len(both) * rows, :] = dot(jnp.concatenate(both, axis=0), zavg[...])

    def coarse_rows(first_row, count):
        return pair[pl.ds(first_row, count, stride=2), :] + pair[pl.ds(first_row + 1, count, stride=2), :]

    def bricks(rows, offset, skip):
        return jnp.concatenate([coarse_rows(rows * (i + skip) + offset, 8) for i in range(8)], axis=0)

    def coarse_force(rows, offset):
        v = jnp.concatenate([coarse_rows(rows * i + offset, 16) for i in range(12)], axis=0)
        v = v.reshape(12, 16, 128)
        c = v[1:-1]
        m = c * (c * c - 1.0) - 0.25 * around3(v)
        co[...] = 0.25 * around3(m)
        return jnp.concatenate([co[i, 2:10, :] for i in range(8)], axis=0)

    average([start[x + 2] for x in range(24)], 32)
    cb[0] = bricks(32, 8, 2)
    g0 = coarse_force(32, 4)
    place(us, u21, bb, urx, ury, urc)
    potential(u21, mu, 22, 8)

    def fourth(x):
        f = around(mu[x + 1], mu[x], mu[x + 2])
        f21[x] = f
        u22[x] = u21[x + 2] + HALF * f + bb[x]

    loop(20, fourth, 10)
    potential(u22, mu, 18, 9)

    def fifth(x):
        f2 = around(mu[x + 1], mu[x], mu[x + 2])
        f0, f1 = fs[x + 4], f21[x + 2]
        j0[x] = DT * (W[0][0] * f0 + W[0][1] * f1 + W[0][2] * f2)
        j1[x] = DT * (W[1][0] * f0 + W[1][1] * f1 + W[1][2] * f2)

    loop(16, fifth, 8)
    average([u21[x] for x in range(24)], 24)
    cb[1] = bricks(24, 4, 2)
    g1 = coarse_force(24, 0)
    average([u22[x + 2] for x in range(16)], 24)
    cb[2] = bricks(24, 4, 0)
    average([j0[x] for x in range(16)], 24)
    part0 = bricks(24, 4, 0)
    average([j1[x] for x in range(16)], 24)
    part1 = bricks(24, 4, 0)
    part0 = part0 + jnp.where(n == 0, cb[0], -HALF * g0)
    part1 = part1 - HALF * g1
    turned = jnp.transpose(jnp.concatenate([part0, part1], axis=0))
    xext[32:160, :] = turned
    xext[0:32, :] = turned[96:128]
    xext[160:192, :] = turned[0:32]

    block = a * 4 + b

    def chain_device(p):
        t, x = lax.rem(p, 8), 2 * (p // 8)
        return (t, x, lax.rem(x + t // 4 + t, 4))

    is_chain = jnp.logical_and(lax.rem(a, 2) == 0, b == lax.rem(a + n // 4 + n, 4))
    me = n + 8 * (a // 2)
    mine = jnp.where(is_chain, me, -1)
    late = lax.rem(n, 4) // 2

    for c, (low, length) in enumerate(((0, 40), (8, 24))):

        @pl.when(late == c)
        def _():
            def each(p):
                src = xext.at[pl.ds(pl.multiple_of(8 * p + 16 + low, 8), length), :]
                dst = gath.at[n, block, pl.ds(low, length), :]

                @pl.when(p != mine)
                def _():
                    send(src, dst, g_s, g_r.at[n], chain_device(p))

                @pl.when(p == mine)
                def _():
                    pltpu.make_async_copy(src, dst, g_r.at[n]).start()

            loop(16, each)

    lane = lax.broadcasted_iota(jnp.int32, (8, 128), 1)
    inner = lane & 7

    def chain_lap(ref, lo, hi, put):
        for r in range(lo, hi, 8):
            c = [ref[t, r : r + 8, :] for t in range(8)]
            turn = lambda by: [pltpu.roll(v, by % 128, 1) for v in c]
            xp, xm, yp, ym, yu, yd = (turn(by) for by in (-8, 8, -1, 1, 7, -7))
            for t in range(8):
                o, up, down = (t + 4) % 8, t // 4 * 4 + (t + 1) % 4, t // 4 * 4 + (t + 3) % 4
                s = jnp.where(lane < 120, xp[t], xp[o]) + jnp.where(lane >= 8, xm[t], xm[o])
                s = s + (jnp.where(inner < 7, yp[t], yu[up]) + jnp.where(inner > 0, ym[t], yd[down]))
                s = s + (ref[t, r + 1 : r + 9, :] + ref[t, r - 1 : r + 7, :])
                put(t, r, c[t], 0.25 * (s - 6.0 * c[t]))

    @pl.when(is_chain)
    def _():
        v0[...] = jnp.zeros_like(v0)

        def sweep(src, dst, m, first, inside, outside):
            def one(t, r, u, l):
                m0[t, r : r + 8, :] = u * (u * u - 1.0) - l

            def two(t, r, u, f):
                x, y = t // 4, t % 4
                rows = pl.ds(r - 8, 8)
                e, o = gath[m, 8 * x + y, rows, :], gath[m, 8 * x + 4 + y, rows, :]
                if first:
                    part = jnp.where(lane < 64, e, pltpu.roll(o, 64, 1))
                else:
                    part = jnp.where(lane < 64, pltpu.roll(e, 64, 1), o)
                dst[t, r : r + 8, :] = src[t, r : r + 8, :] + HALF * f + part

            chain_lap(src, *inside, one)
            chain_lap(m0, *outside, two)

        full, part, core = (8, 48), (16, 40), (24, 32)
        spans = (
            (full, full, full, full),
            (full, full, full, part),
            (part, part, part, part),
            (part, part, part, core),
        )

        def other(d, k):
            p = lax.rem(me + d + 16, 16)
            return pltpu.make_async_remote_copy(
                src_ref=stage.at[3, :, 2], dst_ref=seam.at[k], send_sem=x_s.at[k], recv_sem=x_r.at[k],
                device_id=chain_device(p), device_id_type=MESH,
            )

        seams = [other(d, k) for k, d in ((0, 2), (1, 1), (3, -1), (4, -2))]

        def scatter(m):
            def each(d):
                x, y = d // 4, lax.rem(d, 4)
                src = stage.at[m, (x // 2) * 4 + y]
                dst = back.at[:, pl.ds(pl.multiple_of(8 * me, 8), 8), :]
                own = jnp.logical_and(m == n, d == block)

                @pl.when(jnp.logical_not(own))
                def _():
                    send(src, dst, b_s, b_r, (m, x, y))

                @pl.when(own)
                def _():
                    pltpu.make_async_copy(src, dst, b_r).start()

            loop(16, each)

        def phase(h):
            @pl.when(h == 1)
            def _():
                for copy in seams:
                    copy.start()
                for m in range(4):
                    scatter(m)
                for copy in seams:
                    copy.wait()
                for k in (0, 1, 3, 4):
                    v0[:, 8 + 8 * k : 16 + 8 * k, :] = seam[k]

            for i in range(4):
                m = 4 * h + i
                low, length = ((0, 40), (8, 24))[i // 2]
                whole = gath.at[m, :, pl.ds(low, length), :]
                pltpu.make_async_copy(whole, whole, g_r.at[m]).wait()
                stage[m, :, 0] = v0[:, 24:32, :]
                sweep(v0, v1, m, True, *spans[i][:2])
                stage[m, :, 1] = v1[:, 24:32, :]
                sweep(v1, v0, m, False, *spans[i][2:])
                stage[m, :, 2] = v0[:, 24:32, :]

                @pl.when(h == 1)
                def _():
                    scatter(m)

        loop(2, phase)

    pltpu.make_async_copy(back, back, b_r).wait()
    for j in range(3):
        half[...] = jnp.transpose(back[j])
        rows = pl.ds(pl.multiple_of(64 * lax.rem(a, 2), 64), 64)
        change = half[rows, :] - cb[j]
        if j == 0:
            change = jnp.where(n == 0, 0.0, change)
        fine = dot(dot(ydup[...], change), zdup[...])
        for i in range(8):
            add = fine[16 * i : 16 * i + 16]
            for x in (2 * i, 2 * i + 1):
                if j == 0:
                    node = start[x + 6, 8:24, :]
                elif j == 1:
                    node = u21[x + 4, 4:20, :]
                else:
                    node = u22[x + 2, 4:20, :]
                out[j, 0, x] = node + add

    @pl.when(n < 7)
    def _():
        along.wait_send()

    for copy in raws + ks + starts + us:
        copy.wait_send()
    for c, (low, length) in enumerate(((0, 40), (8, 24))):

        @pl.when(late == c)
        def _():
            @pl.when(is_chain)
            def _():
                sent = gath.at[0, 0:15, pl.ds(low, length), :]
                pltpu.make_async_copy(sent, sent, g_s).wait()

            @pl.when(jnp.logical_not(is_chain))
            def _():
                sent = gath.at[0, :, pl.ds(low, length), :]
                pltpu.make_async_copy(sent, sent, g_s).wait()

    @pl.when(is_chain)
    def _():
        for m in range(8):
            count = stage.at[m]
            if m == 0:
                count = stage.at[0, 0:7]
            pltpu.make_async_copy(count, count, b_s).wait()
        for m in range(8):
            pltpu.make_async_copy(stage.at[m], stage.at[m], b_s).wait()


def local(guess):
    vm = lambda *s: pltpu.VMEM(s, F32)
    dma = lambda *s: pltpu.SemaphoreType.DMA(s)
    vspec = pl.BlockSpec(memory_space=pltpu.VMEM)
    return pl.pallas_call(
        kernel,
        out_shape=jax.ShapeDtypeStruct(guess.shape, F32),
        in_specs=[pl.BlockSpec(memory_space=pl.ANY)],
        out_specs=vspec,
        scratch_shapes=[
            vm(256, 128), vm(128, 256), vm(128, 64),
            vm(3, 20, 32, 256), vm(2, 16, 8, 256), vm(2, 16, 8, 256), vm(4, 1, 8, 256),
            vm(2, 20, 24, 256), vm(2, 20, 24, 256), vm(22, 24, 256), vm(22, 24, 256),
            vm(28, 32, 256), vm(24, 24, 256), vm(20, 24, 256),
            vm(2, 6, 16, 256), vm(2, 6, 16, 256), vm(2, 16, 8, 256), vm(2, 16, 8, 256), vm(4, 3, 8, 256),
            vm(24, 24, 256), vm(20, 24, 256), vm(24, 24, 256), vm(20, 24, 256),
            vm(2, 6, 16, 256), vm(2, 6, 16, 256), vm(2, 16, 8, 256), vm(2, 16, 8, 256), vm(4, 3, 8, 256),
            vm(20, 24, 256),
            vm(24, 24, 256), vm(20, 24, 256), vm(20, 24, 256), vm(16, 24, 256), vm(16, 24, 256), vm(26, 32, 256),
            vm(400, 128), vm(8, 16, 128), vm(3, 64, 128), vm(192, 128),
            vm(8, 16, 40, 128), vm(8, 56, 128), vm(8, 56, 128), vm(8, 56, 128), vm(5, 8, 8, 128),
            vm(8, 8, 3, 8, 128), vm(3, 128, 128), vm(128, 128),
            dma(3), pltpu.SemaphoreType.DMA, pltpu.SemaphoreType.DMA,
            dma(8), dma(8), dma(8), dma(8), dma(8), dma(8), dma(8), dma(8),
            pltpu.SemaphoreType.DMA, dma(8), dma(5), dma(5),
            pltpu.SemaphoreType.DMA, pltpu.SemaphoreType.DMA,
        ],
        compiler_params=pltpu.CompilerParams(
            collective_id=0, has_side_effects=True, vmem_limit_bytes=48 * 1024 * 1024
        ),
    )(guess)


def solution(mesh):
    spec = P(None, "tm", "gx", "gy", None)
    return jax.shard_map(local, mesh=mesh, in_specs=(spec,), out_specs=spec, check_vma=False)
```

```python
import jax
import jax.numpy as jnp
from jax import lax
from jax.experimental import pallas as pl
from jax.experimental.pallas import tpu as pltpu
from jax.sharding import PartitionSpec as P

DT = 0.01
HALF = 0.005
W = ((5.0 / 24.0, 1.0 / 3.0, -1.0 / 24.0), (-1.0 / 24.0, 1.0 / 3.0, 5.0 / 24.0))
OLD = (
    (DT * (W[0][0] - 0.5), DT * W[0][1], DT * W[0][2]),
    (DT * W[1][0], DT * (W[1][1] - 0.5), DT * W[1][2]),
)
MESH = pl.DeviceIdType.MESH
DIRS = ((1, 0), (-1, 0), (0, 1), (0, -1), (1, 1), (1, -1), (-1, 1), (-1, -1))
F32 = jnp.float32
HIGH = lax.Precision.HIGHEST


def dot(a, b):
    return jnp.dot(a, b, precision=HIGH, preferred_element_type=F32)


def around(c, low, high):
    rows, z = c.shape
    s = (low + high) + (pltpu.roll(c, 1, 0) + pltpu.roll(c, rows - 1, 0))
    s = s + (pltpu.roll(c, 1, 1) + pltpu.roll(c, z - 1, 1))
    return s - 6.0 * c


def around3(v):
    c = v[1:-1]
    rows, z = c.shape[1:]
    s = v[:-2] + v[2:] + pltpu.roll(c, 1, 1) + pltpu.roll(c, rows - 1, 1)
    s = s + pltpu.roll(c, 1, 2) + pltpu.roll(c, z - 1, 2)
    return s - 6.0 * c


def loop(count, body, group=1):
    def step(i, carry):
        base = jnp.minimum(group * i, count - group)
        for k in range(group):
            body(base + k)
        return carry

    lax.fori_loop(0, -(-count // group), step, 0)


def potential(src, mu, count, group):
    def body(x):
        c = src[x + 1]
        mu[x] = c * (c * c - 1.0) - around(c, src[x], src[x + 2])

    loop(count, body, group)


def crop(v):
    return pltpu.roll(v, 28, 0)[0:24]


def edge(h, d):
    return pl.ds(16 - h, h) if d > 0 else pl.ds(0, h)


def halo(h, d, at):
    return pl.ds(at - h, h) if d > 0 else pl.ds(at + 16, h)


CORNER = ((1, 0, 5), (4, 5, 2), (2, 8, 4), (3, 12, 3), (5, 15, 1))


def pack_corner(field, packed, k):
    dx, dy = DIRS[4 + k]
    for d, row, count in CORNER:
        x = 22 - d if dx > 0 else 5 + d
        y = 24 - count if dy > 0 else 8
        packed[..., k, row : row + count, :] = field[..., x, y : y + count, :]


def unpack_corner(field, packed, k):
    dx, dy = DIRS[4 + k]
    for d, row, count in CORNER:
        x = 6 - d if dx > 0 else 21 + d
        y = 8 - count if dy > 0 else 24
        field[..., x, y : y + count, :] = packed[..., k, row : row + count, :]


def kernel(
    g, out,
    zavg, zdup, ydup, raw, rsy, rry, rrc, q, w, mu, mu2,
    start, ssc, src_c, k0, k1, ksx, krx, ksy, kry, ksc, krc,
    u11, u12, u21, bb, usx, urx, usy, ury, usc, urc, u22,
    fs, f11, f21, j0, j1, wide,
    pair, co, cb, xext, gath, v0, v1, m0, seam, stage, back, half,
    in_s, st_s, st_r, raw_s, raw_r, k_s, k_r, s_s, s_r, u_s, u_r, g_s, g_r, x_s, x_r, b_s, b_r,
):
    n, a, b = lax.axis_index("tm"), lax.axis_index("gx"), lax.axis_index("gy")

    def at(dt, dx, dy):
        return (lax.rem(n + dt + 8, 8), lax.rem(a + dx + 4, 4), lax.rem(b + dy + 4, 4))

    barrier = pltpu.get_barrier_semaphore()
    for dx, dy in DIRS:
        pl.semaphore_signal(barrier, inc=1, device_id=at(0, dx, dy), device_id_type=MESH)
    for dt in range(1, 8):
        pl.semaphore_signal(barrier, inc=1, device_id=at(dt, 0, 0), device_id_type=MESH)

    block16 = (pl.ds(2, 16), pl.ds(8, 16))
    loads = [pltpu.make_async_copy(g.at[j, 0], raw.at[j, *block16], in_s.at[j]) for j in range(3)]
    for load in loads:
        load.start()

    def iota(shape, d):
        return lax.broadcasted_iota(jnp.int32, shape, d)

    zavg[...] = jnp.where(iota((256, 128), 0) // 2 == iota((256, 128), 1), 0.5, 0.0)
    zdup[...] = jnp.where(iota((128, 256), 0) == iota((128, 256), 1) // 2, 1.0, 0.0)
    r, k = iota((128, 64), 0), iota((128, 64), 1)
    ydup[...] = jnp.where(k == (r // 16) * 8 + lax.rem(r, 16) // 2, 1.0, 0.0)
    for load in loads:
        load.wait()
    for j in range(3):
        rsy[0, :, 2 * j : 2 * j + 2, :] = raw[j, 2:18, 22:24, :]
        rsy[1, :, 2 * j : 2 * j + 2, :] = raw[j, 2:18, 8:10, :]
    pl.semaphore_wait(barrier, 15)

    def send(src, dst, ss, rs, to):
        copy = pltpu.make_async_remote_copy(
            src_ref=src, dst_ref=dst, send_sem=ss, recv_sem=rs, device_id=to, device_id_type=MESH
        )
        copy.start()
        return copy

    mid = start.at[pl.ds(6, 16), pl.ds(8, 16), :]
    along = pltpu.make_async_remote_copy(
        src_ref=raw.at[2, *block16], dst_ref=mid, send_sem=st_s, recv_sem=st_r,
        device_id=at(1, 0, 0), device_id_type=MESH,
    )

    @pl.when(n < 7)
    def _():
        along.start()

    raws = []
    for k, (dx, dy) in enumerate(DIRS):
        if dy == 0:
            src = raw.at[:, pl.ds(16, 2) if dx > 0 else pl.ds(2, 2), pl.ds(8, 16), :]
            dst = raw.at[:, halo(2, dx, 2), pl.ds(8, 16), :]
        elif dx == 0:
            src, dst = rsy.at[(1 - dy) // 2], rry.at[(1 - dy) // 2]
        else:
            src, dst = rsy.at[(1 - dy) // 2, edge(1, dx)], rrc.at[k - 4]
        raws.append(send(src, dst, raw_s.at[k], raw_r.at[k], at(0, dx, dy)))
    @pl.when(n == 0)
    def _():
        start[6:22, 8:24, :] = raw[0, 2:18, 8:24, :]

    @pl.when(n > 0)
    def _():
        along.wait_recv()

    for k in range(4):
        pack_corner(start, ssc, k)
    starts = []
    for k, (dx, dy) in enumerate(DIRS):
        if dx == 0:
            xs = xd = pl.ds(6, 16)
        else:
            xs, xd = (pl.ds(16, 6), pl.ds(0, 6)) if dx > 0 else (pl.ds(6, 6), pl.ds(22, 6))
        if dy == 0:
            ys = yd = pl.ds(8, 16)
        else:
            ys, yd = (pl.ds(16, 8), pl.ds(0, 8)) if dy > 0 else (pl.ds(8, 8), pl.ds(24, 8))
        if k < 4:
            src, dst = start.at[xs, ys], start.at[xd, yd]
        else:
            src, dst = ssc.at[k - 4], src_c.at[k - 4]
        starts.append(send(src, dst, s_s.at[k], s_r.at[k], at(0, dx, dy)))
    for copy in raws:
        copy.wait_recv()
    for s, row in ((0, 6), (1, 24)):
        for j in range(3):
            raw[j, 2:18, row : row + 2, :] = rry[s, :, 2 * j : 2 * j + 2, :]
            for e, x in ((0, 1), (2, 18)):
                raw[j, x, row : row + 2, :] = rrc[e + s, 0, 2 * j : 2 * j + 2, :]

    def mix(x):
        u = [raw[j, x] for j in range(3)]
        c = [v * (v * v - 1.0) for v in u]
        for i in range(2):
            q[i, x] = crop(OLD[i][0] * u[0] + OLD[i][1] * u[1] + OLD[i][2] * u[2])
            w[i, x] = crop(OLD[i][0] * c[0] + OLD[i][1] * c[1] + OLD[i][2] * c[2])

    def mix_potential(x):
        for i, m in ((0, mu), (1, mu2)):
            m[x] = w[i, x + 1] - around(q[i, x + 1], q[i, x], q[i, x + 2])

    def mix_force(x):
        k0[x + 4, 4:20, :] = around(mu[x + 1], mu[x], mu[x + 2])[4:20]
        k1[x + 2, 4:20, :] = around(mu2[x + 1], mu2[x], mu2[x + 2])[4:20]

    loop(20, mix, 5)
    loop(18, mix_potential, 6)
    loop(16, mix_force, 4)

    def wide_halo(p, r, xs, xr, ys, yr, cs, cr, ss, rs):
        ys[0, :, 0:4, :] = p[4:20, 16:20, :]
        ys[0, :, 4:6, :] = r[2:18, 18:20, :]
        ys[1, :, 0:4, :] = p[4:20, 4:8, :]
        ys[1, :, 4:6, :] = r[2:18, 4:6, :]
        xs[0, 0:4] = p[16:20, 4:20, :]
        xs[0, 4:6] = r[16:18, 4:20, :]
        xs[1, 0:4] = p[4:8, 4:20, :]
        xs[1, 4:6] = r[2:4, 4:20, :]
        for k, (dx, dy) in enumerate(DIRS[4:]):
            for row, d, count in ((0, 1, 3), (3, 2, 2), (5, 3, 1)):
                x = 20 - d if dx > 0 else 3 + d
                y = 20 - count if dy > 0 else 4
                cs[k, row : row + count, :] = p[x, y : y + count, :]
            cs[k, 6:7, :] = r[17 if dx > 0 else 2, pl.ds(19 if dy > 0 else 4, 1), :]
        copies = []
        for k, (dx, dy) in enumerate(DIRS):
            s = (1 - dy) // 2
            if dy == 0:
                src, dst = xs.at[(1 - dx) // 2], xr.at[(1 - dx) // 2]
            elif dx == 0:
                src, dst = ys.at[s], yr.at[s]
            else:
                src, dst = cs.at[k - 4], cr.at[k - 4]
            copies.append(send(src, dst, ss.at[k], rs.at[k], at(0, dx, dy)))
        return copies

    def place(copies, p, r, xr, yr, cr):
        for copy in copies:
            copy.wait_recv()
        p[0:4, 4:20, :] = xr[0, 0:4]
        r[0:2, 4:20, :] = xr[0, 4:6]
        p[20:24, 4:20, :] = xr[1, 0:4]
        r[18:20, 4:20, :] = xr[1, 4:6]
        for s, low, near in ((0, 0, 2), (1, 20, 20)):
            p[4:20, low : low + 4, :] = yr[s, :, 0:4, :]
            r[2:18, near : near + 2, :] = yr[s, :, 4:6, :]
        for k, (dx, dy) in enumerate(DIRS[4:]):
            for row, d, count in ((0, 1, 3), (3, 2, 2), (5, 3, 1)):
                x = 4 - d if dx > 0 else 19 + d
                y = 4 - count if dy > 0 else 20
                p[x, y : y + count, :] = cr[k, row : row + count, :]
            r[1 if dx > 0 else 18, pl.ds(3 if dy > 0 else 20, 1), :] = cr[k, 6:7, :]

    ks = wide_halo(k0, k1, ksx, krx, ksy, kry, ksc, krc, k_s, k_r)

    for copy in starts:
        copy.wait_recv()
    for k in range(4):
        unpack_corner(start, src_c, k)
    potential(start, wide, 26, 9)
    place(ks, k0, k1, krx, kry, krc)

    def first(x):
        f = around(wide[x + 1], wide[x], wide[x + 2])
        fs[x] = crop(f)
        u11[x] = crop(start[x + 2] + HALF * f) + k0[x]

    loop(24, first, 8)
    potential(u11, mu, 22, 8)

    def second(x):
        f = around(mu[x + 1], mu[x], mu[x + 2])
        f11[x] = f
        u12[x] = u11[x + 2] + HALF * f + k1[x]

    loop(20, second, 10)
    potential(u12, mu, 18, 9)

    def third(x):
        f2 = around(mu[x + 1], mu[x], mu[x + 2])
        f0, f1 = fs[x + 4], f11[x + 2]
        new = crop(start[x + 6]) + DT * (W[0][0] * f0 + W[0][1] * f1 + W[0][2] * f2)
        u21[x + 4, 4:20, :] = new[4:20]
        bb[x + 2, 4:20, :] = (OLD[1][0] * f0 + OLD[1][1] * f1 + OLD[1][2] * f2)[4:20]

    loop(16, third, 8)
    us = wide_halo(u21, bb, usx, urx, usy, ury, usc, urc, u_s, u_r)

    def average(layers, rows):
        both = [(layers[2 * i] + layers[2 * i + 1]) * 0.25 for i in range(len(layers) // 2)]
        pair[0 : len(both) * rows, :] = dot(jnp.concatenate(both, axis=0), zavg[...])

    def coarse_rows(first_row, count):
        return pair[pl.ds(first_row, count, stride=2), :] + pair[pl.ds(first_row + 1, count, stride=2), :]

    def bricks(rows, offset, skip):
        return jnp.concatenate([coarse_rows(rows * (i + skip) + offset, 8) for i in range(8)], axis=0)

    def coarse_force(rows, offset):
        v = jnp.concatenate([coarse_rows(rows * i + offset, 16) for i in range(12)], axis=0)
        v = v.reshape(12, 16, 128)
        c = v[1:-1]
        m = c * (c * c - 1.0) - 0.25 * around3(v)
        co[...] = 0.25 * around3(m)
        return jnp.concatenate([co[i, 2:10, :] for i in range(8)], axis=0)

    average([start[x + 2] for x in range(24)], 32)
    cb[0] = bricks(32, 8, 2)
    g0 = coarse_force(32, 4)
    place(us, u21, bb, urx, ury, urc)
    potential(u21, mu, 22, 8)

    def fourth(x):
        f = around(mu[x + 1], mu[x], mu[x + 2])
        f21[x] = f
        u22[x] = u21[x + 2] + HALF * f + bb[x]

    loop(20, fourth, 10)
    potential(u22, mu, 18, 9)

    def fifth(x):
        f2 = around(mu[x + 1], mu[x], mu[x + 2])
        f0, f1 = fs[x + 4], f21[x + 2]
        j0[x] = DT * (W[0][0] * f0 + W[0][1] * f1 + W[0][2] * f2)
        j1[x] = DT * (W[1][0] * f0 + W[1][1] * f1 + W[1][2] * f2)

    loop(16, fifth, 8)
    average([u21[x] for x in range(24)], 24)
    cb[1] = bricks(24, 4, 2)
    g1 = coarse_force(24, 0)
    average([u22[x + 2] for x in range(16)], 24)
    cb[2] = bricks(24, 4, 0)
    average([j0[x] for x in range(16)], 24)
    part0 = bricks(24, 4, 0)
    average([j1[x] for x in range(16)], 24)
    part1 = bricks(24, 4, 0)
    part0 = part0 + jnp.where(n == 0, cb[0], -HALF * g0)
    part1 = part1 - HALF * g1
    turned = jnp.transpose(jnp.concatenate([part0, part1], axis=0))
    xext[32:160, :] = turned
    xext[0:32, :] = turned[96:128]
    xext[160:192, :] = turned[0:32]

    block = a * 4 + b

    def chain_device(p):
        t, x = lax.rem(p, 8), 2 * (p // 8)
        return (t, x, lax.rem(x + t // 4 + t, 4))

    is_chain = jnp.logical_and(lax.rem(a, 2) == 0, b == lax.rem(a + n // 4 + n, 4))
    me = n + 8 * (a // 2)
    mine = jnp.where(is_chain, me, -1)
    late = lax.rem(n, 4) // 2

    for c, (low, length) in enumerate(((0, 40), (8, 24))):

        @pl.when(late == c)
        def _():
            def part(p):
                src = xext.at[pl.ds(pl.multiple_of(8 * p + 16 + low, 8), length), :]
                return src, gath.at[n, block, pl.ds(low, length), :]

            for p in range(16):

                @pl.when(p != mine)
                def _():
                    send(*part(p), g_s, g_r.at[n], chain_device(p))

            @pl.when(is_chain)
            def _():
                pltpu.make_async_copy(*part(me), g_r.at[n]).start()

    lane = lax.broadcasted_iota(jnp.int32, (8, 128), 1)
    inner = lane & 7

    def chain_lap(ref, lo, hi, put):
        for r in range(lo, hi, 8):
            c = [ref[t, r : r + 8, :] for t in range(8)]
            turn = lambda by: [pltpu.roll(v, by % 128, 1) for v in c]
            xp, xm, yp, ym, yu, yd = (turn(by) for by in (-8, 8, -1, 1, 7, -7))
            for t in range(8):
                o, up, down = (t + 4) % 8, t // 4 * 4 + (t + 1) % 4, t // 4 * 4 + (t + 3) % 4
                s = jnp.where(lane < 120, xp[t], xp[o]) + jnp.where(lane >= 8, xm[t], xm[o])
                s = s + (jnp.where(inner < 7, yp[t], yu[up]) + jnp.where(inner > 0, ym[t], yd[down]))
                s = s + (ref[t, r + 1 : r + 9, :] + ref[t, r - 1 : r + 7, :])
                put(t, r, c[t], 0.25 * (s - 6.0 * c[t]))

    @pl.when(is_chain)
    def _():
        v0[...] = jnp.zeros_like(v0)

        def sweep(src, dst, m, first, inside, outside):
            def one(t, r, u, l):
                m0[t, r : r + 8, :] = u * (u * u - 1.0) - l

            def two(t, r, u, f):
                x, y = t // 4, t % 4
                rows = pl.ds(r - 8, 8)
                e, o = gath[m, 8 * x + y, rows, :], gath[m, 8 * x + 4 + y, rows, :]
                if first:
                    part = jnp.where(lane < 64, e, pltpu.roll(o, 64, 1))
                else:
                    part = jnp.where(lane < 64, pltpu.roll(e, 64, 1), o)
                dst[t, r : r + 8, :] = src[t, r : r + 8, :] + HALF * f + part

            chain_lap(src, *inside, one)
            chain_lap(m0, *outside, two)

        full, part, core = (8, 48), (16, 40), (24, 32)
        spans = (
            (full, full, full, full),
            (full, full, full, part),
            (part, part, part, part),
            (part, part, part, core),
        )

        def other(d, k):
            p = lax.rem(me + d + 16, 16)
            return pltpu.make_async_remote_copy(
                src_ref=stage.at[3, :, 2], dst_ref=seam.at[k], send_sem=x_s.at[k], recv_sem=x_r.at[k],
                device_id=chain_device(p), device_id_type=MESH,
            )

        seams = [other(d, k) for k, d in ((0, 2), (1, 1), (3, -1), (4, -2))]

        def scatter(m):
            for d in range(16):
                to = lax.rem(block + d, 16)
                x, y = to // 4, lax.rem(to, 4)
                src = stage.at[m, (x // 2) * 4 + y]
                dst = back.at[:, pl.ds(pl.multiple_of(8 * me, 8), 8), :]
                if d > 0:
                    send(src, dst, b_s, b_r, (m, x, y))
                else:

                    @pl.when(m != n)
                    def _():
                        send(src, dst, b_s, b_r, (m, x, y))

                    @pl.when(m == n)
                    def _():
                        pltpu.make_async_copy(src, dst, b_r).start()

        def phase(h):
            @pl.when(h == 1)
            def _():
                for copy in seams:
                    copy.start()
                for m in range(4):
                    scatter(m)
                for copy in seams:
                    copy.wait()
                for k in (0, 1, 3, 4):
                    v0[:, 8 + 8 * k : 16 + 8 * k, :] = seam[k]

            for i in range(4):
                m = 4 * h + i
                low, length = ((0, 40), (8, 24))[i // 2]
                whole = gath.at[m, :, pl.ds(low, length), :]
                pltpu.make_async_copy(whole, whole, g_r.at[m]).wait()
                stage[m, :, 0] = v0[:, 24:32, :]
                sweep(v0, v1, m, True, *spans[i][:2])
                stage[m, :, 1] = v1[:, 24:32, :]
                sweep(v1, v0, m, False, *spans[i][2:])
                stage[m, :, 2] = v0[:, 24:32, :]

                @pl.when(h == 1)
                def _():
                    scatter(m)

        loop(2, phase)

    pltpu.make_async_copy(back, back, b_r).wait()
    for j in range(3):
        half[...] = jnp.transpose(back[j])
        rows = pl.ds(pl.multiple_of(64 * lax.rem(a, 2), 64), 64)
        change = half[rows, :] - cb[j]
        if j == 0:
            change = jnp.where(n == 0, 0.0, change)
        fine = dot(dot(ydup[...], change), zdup[...])
        for i in range(8):
            add = fine[16 * i : 16 * i + 16]
            for x in (2 * i, 2 * i + 1):
                if j == 0:
                    node = start[x + 6, 8:24, :]
                elif j == 1:
                    node = u21[x + 4, 4:20, :]
                else:
                    node = u22[x + 2, 4:20, :]
                out[j, 0, x] = node + add

    @pl.when(n < 7)
    def _():
        along.wait_send()

    for copy in raws + ks + starts + us:
        copy.wait_send()
    for c, (low, length) in enumerate(((0, 40), (8, 24))):

        @pl.when(late == c)
        def _():
            @pl.when(is_chain)
            def _():
                sent = gath.at[0, 0:15, pl.ds(low, length), :]
                pltpu.make_async_copy(sent, sent, g_s).wait()

            @pl.when(jnp.logical_not(is_chain))
            def _():
                sent = gath.at[0, :, pl.ds(low, length), :]
                pltpu.make_async_copy(sent, sent, g_s).wait()

    @pl.when(is_chain)
    def _():
        for m in range(8):
            count = stage.at[m]
            if m == 0:
                count = stage.at[0, 0:7]
            pltpu.make_async_copy(count, count, b_s).wait()
        for m in range(8):
            pltpu.make_async_copy(stage.at[m], stage.at[m], b_s).wait()


def local(guess):
    vm = lambda *s: pltpu.VMEM(s, F32)
    dma = lambda *s: pltpu.SemaphoreType.DMA(s)
    vspec = pl.BlockSpec(memory_space=pltpu.VMEM)
    return pl.pallas_call(
        kernel,
        out_shape=jax.ShapeDtypeStruct(guess.shape, F32),
        in_specs=[pl.BlockSpec(memory_space=pl.ANY)],
        out_specs=vspec,
        scratch_shapes=[
            vm(256, 128), vm(128, 256), vm(128, 64),
            vm(3, 20, 32, 256), vm(2, 16, 8, 256), vm(2, 16, 8, 256), vm(4, 1, 8, 256),
            vm(2, 20, 24, 256), vm(2, 20, 24, 256), vm(22, 24, 256), vm(22, 24, 256),
            vm(28, 32, 256), vm(4, 16, 256), vm(4, 16, 256), vm(24, 24, 256), vm(20, 24, 256),
            vm(2, 6, 16, 256), vm(2, 6, 16, 256), vm(2, 16, 8, 256), vm(2, 16, 8, 256), vm(4, 8, 256), vm(4, 8, 256),
            vm(24, 24, 256), vm(20, 24, 256), vm(24, 24, 256), vm(20, 24, 256),
            vm(2, 6, 16, 256), vm(2, 6, 16, 256), vm(2, 16, 8, 256), vm(2, 16, 8, 256), vm(4, 8, 256), vm(4, 8, 256),
            vm(20, 24, 256),
            vm(24, 24, 256), vm(20, 24, 256), vm(20, 24, 256), vm(16, 24, 256), vm(16, 24, 256), vm(26, 32, 256),
            vm(400, 128), vm(8, 16, 128), vm(3, 64, 128), vm(192, 128),
            vm(8, 16, 40, 128), vm(8, 56, 128), vm(8, 56, 128), vm(8, 56, 128), vm(5, 8, 8, 128),
            vm(8, 8, 3, 8, 128), vm(3, 128, 128), vm(128, 128),
            dma(3), pltpu.SemaphoreType.DMA, pltpu.SemaphoreType.DMA,
            dma(8), dma(8), dma(8), dma(8), dma(8), dma(8), dma(8), dma(8),
            pltpu.SemaphoreType.DMA, dma(8), dma(5), dma(5),
            pltpu.SemaphoreType.DMA, pltpu.SemaphoreType.DMA,
        ],
        compiler_params=pltpu.CompilerParams(
            collective_id=0, has_side_effects=True, vmem_limit_bytes=48 * 1024 * 1024
        ),
    )(guess)


def solution(mesh):
    spec = P(None, "tm", "gx", "gy", None)
    return jax.shard_map(local, mesh=mesh, in_specs=(spec,), out_specs=spec, check_vma=False)
```

```python
import jax
import jax.numpy as jnp
from jax import lax
from jax.experimental import pallas as pl
from jax.experimental.pallas import tpu as pltpu
from jax.sharding import PartitionSpec as P

DT = 0.01
HALF = 0.005
W = ((5.0 / 24.0, 1.0 / 3.0, -1.0 / 24.0), (-1.0 / 24.0, 1.0 / 3.0, 5.0 / 24.0))
OLD = (
    (DT * (W[0][0] - 0.5), DT * W[0][1], DT * W[0][2]),
    (DT * W[1][0], DT * (W[1][1] - 0.5), DT * W[1][2]),
)
MESH = pl.DeviceIdType.MESH
DIRS = ((1, 0), (-1, 0), (0, 1), (0, -1), (1, 1), (1, -1), (-1, 1), (-1, -1))
F32 = jnp.float32
HIGH = lax.Precision.HIGHEST


def dot(a, b):
    return jnp.dot(a, b, precision=HIGH, preferred_element_type=F32)


def around(c, low, high):
    rows, z = c.shape
    s = (low + high) + (pltpu.roll(c, 1, 0) + pltpu.roll(c, rows - 1, 0))
    s = s + (pltpu.roll(c, 1, 1) + pltpu.roll(c, z - 1, 1))
    return s - 6.0 * c


def around3(v):
    c = v[1:-1]
    rows, z = c.shape[1:]
    s = v[:-2] + v[2:] + pltpu.roll(c, 1, 1) + pltpu.roll(c, rows - 1, 1)
    s = s + pltpu.roll(c, 1, 2) + pltpu.roll(c, z - 1, 2)
    return s - 6.0 * c


def loop(count, body, group=1):
    def step(i, carry):
        base = jnp.minimum(group * i, count - group)
        for k in range(group):
            body(base + k)
        return carry

    lax.fori_loop(0, -(-count // group), step, 0)


def potential(src, mu, count, group):
    def body(x):
        c = src[x + 1]
        mu[x] = c * (c * c - 1.0) - around(c, src[x], src[x + 2])

    loop(count, body, group)


def crop(v):
    return pltpu.roll(v, 28, 0)[0:24]


def edge(h, d):
    return pl.ds(16 - h, h) if d > 0 else pl.ds(0, h)


def halo(h, d, at):
    return pl.ds(at - h, h) if d > 0 else pl.ds(at + 16, h)


CORNER = ((1, 0, 5), (4, 5, 2), (2, 8, 4), (3, 12, 3), (5, 15, 1))


def pack_corner(field, packed, k):
    dx, dy = DIRS[4 + k]
    for d, row, count in CORNER:
        x = 22 - d if dx > 0 else 5 + d
        y = 24 - count if dy > 0 else 8
        packed[..., k, row : row + count, :] = field[..., x, y : y + count, :]


def unpack_corner(field, packed, k):
    dx, dy = DIRS[4 + k]
    for d, row, count in CORNER:
        x = 6 - d if dx > 0 else 21 + d
        y = 8 - count if dy > 0 else 24
        field[..., x, y : y + count, :] = packed[..., k, row : row + count, :]


def kernel(
    g, out,
    zavg, zdup, ydup, raw, rsy, rry, rrc, q, w, mu, mu2,
    start, ssc, src_c, k0, k1, ksx, krx, ksy, kry, ksc, krc,
    u11, u12, u21, bb, usx, urx, usy, ury, usc, urc, u22,
    fs, f11, f21, j0, j1, wide,
    pair, co, cb, xext, gath, v0, v1, m0, seam, stage, back, half,
    in_s, st_s, st_r, raw_s, raw_r, k_s, k_r, s_s, s_r, u_s, u_r, g_s, g_r, x_s, x_r, b_s, b_r,
):
    n, a, b = lax.axis_index("tm"), lax.axis_index("gx"), lax.axis_index("gy")

    def at(dt, dx, dy):
        return (lax.rem(n + dt + 8, 8), lax.rem(a + dx + 4, 4), lax.rem(b + dy + 4, 4))

    barrier = pltpu.get_barrier_semaphore()
    for dx, dy in DIRS:
        pl.semaphore_signal(barrier, inc=1, device_id=at(0, dx, dy), device_id_type=MESH)
    for dt in range(1, 8):
        pl.semaphore_signal(barrier, inc=1, device_id=at(dt, 0, 0), device_id_type=MESH)

    block16 = (pl.ds(2, 16), pl.ds(8, 16))
    loads = [pltpu.make_async_copy(g.at[j, 0], raw.at[j, *block16], in_s.at[j]) for j in range(3)]
    for load in loads:
        load.start()

    def iota(shape, d):
        return lax.broadcasted_iota(jnp.int32, shape, d)

    zavg[...] = jnp.where(iota((256, 128), 0) // 2 == iota((256, 128), 1), 0.5, 0.0)
    zdup[...] = jnp.where(iota((128, 256), 0) == iota((128, 256), 1) // 2, 1.0, 0.0)
    r, k = iota((128, 64), 0), iota((128, 64), 1)
    ydup[...] = jnp.where(k == (r // 16) * 8 + lax.rem(r, 16) // 2, 1.0, 0.0)
    for load in loads:
        load.wait()
    for j in range(3):
        rsy[0, :, 2 * j : 2 * j + 2, :] = raw[j, 2:18, 22:24, :]
        rsy[1, :, 2 * j : 2 * j + 2, :] = raw[j, 2:18, 8:10, :]
    pl.semaphore_wait(barrier, 15)

    def send(src, dst, ss, rs, to):
        copy = pltpu.make_async_remote_copy(
            src_ref=src, dst_ref=dst, send_sem=ss, recv_sem=rs, device_id=to, device_id_type=MESH
        )
        copy.start()
        return copy

    along = [
        pltpu.make_async_remote_copy(
            src_ref=raw.at[2, pl.ds(2 + 8 * h, 8), pl.ds(8, 16)],
            dst_ref=start.at[pl.ds(6 + 8 * h, 8), pl.ds(8, 16)],
            send_sem=st_s.at[h], recv_sem=st_r.at[h], device_id=at(1, 0, 0), device_id_type=MESH,
        )
        for h in range(2)
    ]

    @pl.when(n < 7)
    def _():
        for copy in along:
            copy.start()

    raws = []
    for k, (dx, dy) in enumerate(DIRS):
        if dy == 0:
            src = raw.at[:, pl.ds(16, 2) if dx > 0 else pl.ds(2, 2), pl.ds(8, 16), :]
            dst = raw.at[:, halo(2, dx, 2), pl.ds(8, 16), :]
        elif dx == 0:
            src, dst = rsy.at[(1 - dy) // 2], rry.at[(1 - dy) // 2]
        else:
            src, dst = rsy.at[(1 - dy) // 2, edge(1, dx)], rrc.at[k - 4]
        raws.append(send(src, dst, raw_s.at[k], raw_r.at[k], at(0, dx, dy)))
    @pl.when(n == 0)
    def _():
        start[6:22, 8:24, :] = raw[0, 2:18, 8:24, :]

    starts = []
    for h in range(2):

        @pl.when(n > 0)
        def _():
            along[h].wait_recv()

        layers = pl.ds(6 + 8 * h, 8)
        for k, (dx, dy) in enumerate(DIRS):
            if dx == (1, -1)[h]:
                continue
            to, slot = at(0, dx, dy), k + 10 * h if dx == 0 else k
            if dx == 0:
                ys, yd = (pl.ds(16, 8), pl.ds(0, 8)) if dy > 0 else (pl.ds(8, 8), pl.ds(24, 8))
                src, dst = start.at[layers, ys], start.at[layers, yd]
            elif dy == 0:
                xs, xd = (pl.ds(16, 6), pl.ds(0, 6)) if dx > 0 else (pl.ds(6, 6), pl.ds(22, 6))
                src, dst = start.at[xs, pl.ds(8, 16)], start.at[xd, pl.ds(8, 16)]
            else:
                pack_corner(start, ssc, k - 4)
                src, dst = ssc.at[k - 4], src_c.at[k - 4]
            starts.append(send(src, dst, s_s.at[slot], s_r.at[slot], to))
    for copy in raws:
        copy.wait_recv()
    for s, row in ((0, 6), (1, 24)):
        for j in range(3):
            raw[j, 2:18, row : row + 2, :] = rry[s, :, 2 * j : 2 * j + 2, :]
            for e, x in ((0, 1), (2, 18)):
                raw[j, x, row : row + 2, :] = rrc[e + s, 0, 2 * j : 2 * j + 2, :]

    def mix(x):
        u = [raw[j, x] for j in range(3)]
        c = [v * (v * v - 1.0) for v in u]
        for i in range(2):
            q[i, x] = crop(OLD[i][0] * u[0] + OLD[i][1] * u[1] + OLD[i][2] * u[2])
            w[i, x] = crop(OLD[i][0] * c[0] + OLD[i][1] * c[1] + OLD[i][2] * c[2])

    def mix_potential(x):
        for i, m in ((0, mu), (1, mu2)):
            m[x] = w[i, x + 1] - around(q[i, x + 1], q[i, x], q[i, x + 2])

    def mix_force(x):
        k0[x + 4, 4:20, :] = around(mu[x + 1], mu[x], mu[x + 2])[4:20]
        k1[x + 2, 4:20, :] = around(mu2[x + 1], mu2[x], mu2[x + 2])[4:20]

    loop(20, mix, 5)
    loop(18, mix_potential, 6)
    loop(16, mix_force, 4)

    def wide_halo(p, r, xs, xr, ys, yr, cs, cr, ss, rs):
        ys[0, :, 0:4, :] = p[4:20, 16:20, :]
        ys[0, :, 4:6, :] = r[2:18, 18:20, :]
        ys[1, :, 0:4, :] = p[4:20, 4:8, :]
        ys[1, :, 4:6, :] = r[2:18, 4:6, :]
        xs[0, 0:4] = p[16:20, 4:20, :]
        xs[0, 4:6] = r[16:18, 4:20, :]
        xs[1, 0:4] = p[4:8, 4:20, :]
        xs[1, 4:6] = r[2:4, 4:20, :]
        for k, (dx, dy) in enumerate(DIRS[4:]):
            for row, d, count in ((0, 1, 3), (3, 2, 2), (5, 3, 1)):
                x = 20 - d if dx > 0 else 3 + d
                y = 20 - count if dy > 0 else 4
                cs[k, row : row + count, :] = p[x, y : y + count, :]
            cs[k, 6:7, :] = r[17 if dx > 0 else 2, pl.ds(19 if dy > 0 else 4, 1), :]
        copies = []
        for k, (dx, dy) in enumerate(DIRS):
            s = (1 - dy) // 2
            if dy == 0:
                src, dst = xs.at[(1 - dx) // 2], xr.at[(1 - dx) // 2]
            elif dx == 0:
                src, dst = ys.at[s], yr.at[s]
            else:
                src, dst = cs.at[k - 4], cr.at[k - 4]
            copies.append(send(src, dst, ss.at[k], rs.at[k], at(0, dx, dy)))
        return copies

    def place(copies, p, r, xr, yr, cr):
        for copy in copies:
            copy.wait_recv()
        p[0:4, 4:20, :] = xr[0, 0:4]
        r[0:2, 4:20, :] = xr[0, 4:6]
        p[20:24, 4:20, :] = xr[1, 0:4]
        r[18:20, 4:20, :] = xr[1, 4:6]
        for s, low, near in ((0, 0, 2), (1, 20, 20)):
            p[4:20, low : low + 4, :] = yr[s, :, 0:4, :]
            r[2:18, near : near + 2, :] = yr[s, :, 4:6, :]
        for k, (dx, dy) in enumerate(DIRS[4:]):
            for row, d, count in ((0, 1, 3), (3, 2, 2), (5, 3, 1)):
                x = 4 - d if dx > 0 else 19 + d
                y = 4 - count if dy > 0 else 20
                p[x, y : y + count, :] = cr[k, row : row + count, :]
            r[1 if dx > 0 else 18, pl.ds(3 if dy > 0 else 20, 1), :] = cr[k, 6:7, :]

    ks = wide_halo(k0, k1, ksx, krx, ksy, kry, ksc, krc, k_s, k_r)

    for copy in starts:
        copy.wait_recv()
    for k in range(4):
        unpack_corner(start, src_c, k)
    potential(start, wide, 26, 9)
    place(ks, k0, k1, krx, kry, krc)

    def first(x):
        f = around(wide[x + 1], wide[x], wide[x + 2])
        fs[x] = crop(f)
        u11[x] = crop(start[x + 2] + HALF * f) + k0[x]

    loop(24, first, 8)
    potential(u11, mu, 22, 8)

    def second(x):
        f = around(mu[x + 1], mu[x], mu[x + 2])
        f11[x] = f
        u12[x] = u11[x + 2] + HALF * f + k1[x]

    loop(20, second, 10)
    potential(u12, mu, 18, 9)

    def third(x):
        f2 = around(mu[x + 1], mu[x], mu[x + 2])
        f0, f1 = fs[x + 4], f11[x + 2]
        new = crop(start[x + 6]) + DT * (W[0][0] * f0 + W[0][1] * f1 + W[0][2] * f2)
        u21[x + 4, 4:20, :] = new[4:20]
        bb[x + 2, 4:20, :] = (OLD[1][0] * f0 + OLD[1][1] * f1 + OLD[1][2] * f2)[4:20]

    loop(16, third, 8)
    us = wide_halo(u21, bb, usx, urx, usy, ury, usc, urc, u_s, u_r)

    def average(layers, rows):
        both = [(layers[2 * i] + layers[2 * i + 1]) * 0.25 for i in range(len(layers) // 2)]
        pair[0 : len(both) * rows, :] = dot(jnp.concatenate(both, axis=0), zavg[...])

    def coarse_rows(first_row, count):
        return pair[pl.ds(first_row, count, stride=2), :] + pair[pl.ds(first_row + 1, count, stride=2), :]

    def bricks(rows, offset, skip):
        return jnp.concatenate([coarse_rows(rows * (i + skip) + offset, 8) for i in range(8)], axis=0)

    def coarse_force(rows, offset):
        v = jnp.concatenate([coarse_rows(rows * i + offset, 16) for i in range(12)], axis=0)
        v = v.reshape(12, 16, 128)
        c = v[1:-1]
        m = c * (c * c - 1.0) - 0.25 * around3(v)
        co[...] = 0.25 * around3(m)
        return jnp.concatenate([co[i, 2:10, :] for i in range(8)], axis=0)

    average([start[x + 2] for x in range(24)], 32)
    cb[0] = bricks(32, 8, 2)
    g0 = coarse_force(32, 4)
    place(us, u21, bb, urx, ury, urc)
    potential(u21, mu, 22, 8)

    def fourth(x):
        f = around(mu[x + 1], mu[x], mu[x + 2])
        f21[x] = f
        u22[x] = u21[x + 2] + HALF * f + bb[x]

    loop(20, fourth, 10)
    potential(u22, mu, 18, 9)

    def fifth(x):
        f2 = around(mu[x + 1], mu[x], mu[x + 2])
        f0, f1 = fs[x + 4], f21[x + 2]
        j0[x] = DT * (W[0][0] * f0 + W[0][1] * f1 + W[0][2] * f2)
        j1[x] = DT * (W[1][0] * f0 + W[1][1] * f1 + W[1][2] * f2)

    loop(16, fifth, 8)
    average([u21[x] for x in range(24)], 24)
    cb[1] = bricks(24, 4, 2)
    g1 = coarse_force(24, 0)
    average([u22[x + 2] for x in range(16)], 24)
    cb[2] = bricks(24, 4, 0)
    average([j0[x] for x in range(16)], 24)
    part0 = bricks(24, 4, 0)
    average([j1[x] for x in range(16)], 24)
    part1 = bricks(24, 4, 0)
    part0 = part0 + jnp.where(n == 0, cb[0], -HALF * g0)
    part1 = part1 - HALF * g1
    turned = jnp.transpose(jnp.concatenate([part0, part1], axis=0))
    xext[32:160, :] = turned
    xext[0:32, :] = turned[96:128]
    xext[160:192, :] = turned[0:32]

    block = a * 4 + b

    def chain_device(p):
        t, x = lax.rem(p, 8), 2 * (p // 8)
        return (t, x, lax.rem(x + t // 4 + t, 4))

    is_chain = jnp.logical_and(lax.rem(a, 2) == 0, b == lax.rem(a + n // 4 + n, 4))
    me = n + 8 * (a // 2)
    mine = jnp.where(is_chain, me, -1)
    late = lax.rem(n, 4) // 2

    for c, (low, length) in enumerate(((0, 40), (8, 24))):

        @pl.when(late == c)
        def _():
            def part(p):
                src = xext.at[pl.ds(pl.multiple_of(8 * p + 16 + low, 8), length), :]
                return src, gath.at[n, block, pl.ds(low, length), :]

            for p in range(16):

                @pl.when(p != mine)
                def _():
                    send(*part(p), g_s, g_r.at[n], chain_device(p))

            @pl.when(is_chain)
            def _():
                pltpu.make_async_copy(*part(me), g_r.at[n]).start()

    lane = lax.broadcasted_iota(jnp.int32, (8, 128), 1)
    inner = lane & 7

    def chain_lap(ref, lo, hi, put):
        for r in range(lo, hi, 8):
            c = [ref[t, r : r + 8, :] for t in range(8)]
            turn = lambda by: [pltpu.roll(v, by % 128, 1) for v in c]
            xp, xm, yp, ym, yu, yd = (turn(by) for by in (-8, 8, -1, 1, 7, -7))
            for t in range(8):
                o, up, down = (t + 4) % 8, t // 4 * 4 + (t + 1) % 4, t // 4 * 4 + (t + 3) % 4
                s = jnp.where(lane < 120, xp[t], xp[o]) + jnp.where(lane >= 8, xm[t], xm[o])
                s = s + (jnp.where(inner < 7, yp[t], yu[up]) + jnp.where(inner > 0, ym[t], yd[down]))
                s = s + (ref[t, r + 1 : r + 9, :] + ref[t, r - 1 : r + 7, :])
                put(t, r, c[t], 0.25 * (s - 6.0 * c[t]))

    @pl.when(is_chain)
    def _():
        v0[...] = jnp.zeros_like(v0)

        def sweep(src, dst, m, first, inside, outside):
            def one(t, r, u, l):
                m0[t, r : r + 8, :] = u * (u * u - 1.0) - l

            def two(t, r, u, f):
                x, y = t // 4, t % 4
                rows = pl.ds(r - 8, 8)
                e, o = gath[m, 8 * x + y, rows, :], gath[m, 8 * x + 4 + y, rows, :]
                if first:
                    part = jnp.where(lane < 64, e, pltpu.roll(o, 64, 1))
                else:
                    part = jnp.where(lane < 64, pltpu.roll(e, 64, 1), o)
                dst[t, r : r + 8, :] = src[t, r : r + 8, :] + HALF * f + part

            chain_lap(src, *inside, one)
            chain_lap(m0, *outside, two)

        full, part, core = (8, 48), (16, 40), (24, 32)
        spans = (
            (full, full, full, full),
            (full, full, full, part),
            (part, part, part, part),
            (part, part, part, core),
        )

        def other(d, k):
            p = lax.rem(me + d + 16, 16)
            return pltpu.make_async_remote_copy(
                src_ref=stage.at[3, 0, :, 1], dst_ref=seam.at[k], send_sem=x_s.at[k], recv_sem=x_r.at[k],
                device_id=chain_device(p), device_id_type=MESH,
            )

        seams = [other(d, k) for k, d in ((0, 2), (1, 1), (3, -1), (4, -2))]

        def scatter(m):
            for d in range(16):
                to = lax.rem(block + d, 16)
                x, y = to // 4, lax.rem(to, 4)
                src = stage.at[m, lax.rem(x, 2), (x // 2) * 4 + y]
                dst = back.at[:, pl.ds(pl.multiple_of(8 * me, 8), 8), :]
                if d > 0:
                    send(src, dst, b_s, b_r, (m, x, y))
                else:

                    @pl.when(m != n)
                    def _():
                        send(src, dst, b_s, b_r, (m, x, y))

                    @pl.when(m == n)
                    def _():
                        pltpu.make_async_copy(src, dst, b_r).start()

        def phase(h):
            @pl.when(h == 1)
            def _():
                for copy in seams:
                    copy.start()
                scatter(3)
                for copy in seams:
                    copy.wait()
                for k in (0, 1, 3, 4):
                    v0[:, 8 + 8 * k : 16 + 8 * k, :] = seam[k]

            for i in range(4):
                m = 4 * h + i
                low, length = ((0, 40), (8, 24))[i // 2]
                whole = gath.at[m, :, pl.ds(low, length), :]
                pltpu.make_async_copy(whole, whole, g_r.at[m]).wait()
                begin = [v0[t, 24:32, :] for t in range(8)]
                sweep(v0, v1, m, True, *spans[i][:2])
                for t in range(8):
                    middle = v1[t, 24:32, :]
                    stage[m, 0, t, 0] = jnp.where(lane < 64, begin[t], pltpu.roll(middle, 64, 1))
                    stage[m, 1, t, 0] = jnp.where(lane < 64, pltpu.roll(begin[t], 64, 1), middle)
                sweep(v1, v0, m, False, *spans[i][2:])
                stage[m, 0, :, 1] = v0[:, 24:32, :]
                stage[m, 1, :, 1] = v0[:, 24:32, :]

                if i < 3:
                    scatter(m)
                else:

                    @pl.when(h == 1)
                    def _():
                        scatter(m)

        loop(2, phase)

    pltpu.make_async_copy(back, back, b_r).wait()
    half[0] = jnp.transpose(back[0])
    half[1] = jnp.transpose(back[1])
    own_half = pl.ds(pl.multiple_of(64 * lax.rem(a, 2), 64), 64)
    for j in range(3):
        change = (half[0, 0:64], half[0, 64:128], half[1, own_half])[j] - cb[j]
        if j == 0:
            change = jnp.where(n == 0, 0.0, change)
        fine = dot(dot(ydup[...], change), zdup[...])
        for i in range(8):
            add = fine[16 * i : 16 * i + 16]
            for x in (2 * i, 2 * i + 1):
                if j == 0:
                    node = start[x + 6, 8:24, :]
                elif j == 1:
                    node = u21[x + 4, 4:20, :]
                else:
                    node = u22[x + 2, 4:20, :]
                out[j, 0, x] = node + add

    @pl.when(n < 7)
    def _():
        for copy in along:
            copy.wait_send()

    for copy in raws + ks + starts + us:
        copy.wait_send()
    for c, (low, length) in enumerate(((0, 40), (8, 24))):

        @pl.when(late == c)
        def _():
            @pl.when(is_chain)
            def _():
                sent = gath.at[0, 0:15, pl.ds(low, length), :]
                pltpu.make_async_copy(sent, sent, g_s).wait()

            @pl.when(jnp.logical_not(is_chain))
            def _():
                sent = gath.at[0, :, pl.ds(low, length), :]
                pltpu.make_async_copy(sent, sent, g_s).wait()

    @pl.when(is_chain)
    def _():
        sent = stage.at[0, 0, 0:7]
        pltpu.make_async_copy(sent, sent, b_s).wait()
        sent = stage.at[0, 1]
        pltpu.make_async_copy(sent, sent, b_s).wait()
        for m in range(1, 8):
            pltpu.make_async_copy(stage.at[m], stage.at[m], b_s).wait()


def local(guess):
    vm = lambda *s: pltpu.VMEM(s, F32)
    dma = lambda *s: pltpu.SemaphoreType.DMA(s)
    vspec = pl.BlockSpec(memory_space=pltpu.VMEM)
    return pl.pallas_call(
        kernel,
        out_shape=jax.ShapeDtypeStruct(guess.shape, F32),
        in_specs=[pl.BlockSpec(memory_space=pl.ANY)],
        out_specs=vspec,
        scratch_shapes=[
            vm(256, 128), vm(128, 256), vm(128, 64),
            vm(3, 20, 32, 256), vm(2, 16, 8, 256), vm(2, 16, 8, 256), vm(4, 1, 8, 256),
            vm(2, 20, 24, 256), vm(2, 20, 24, 256), vm(22, 24, 256), vm(22, 24, 256),
            vm(28, 32, 256), vm(4, 16, 256), vm(4, 16, 256), vm(24, 24, 256), vm(20, 24, 256),
            vm(2, 6, 16, 256), vm(2, 6, 16, 256), vm(2, 16, 8, 256), vm(2, 16, 8, 256), vm(4, 8, 256), vm(4, 8, 256),
            vm(24, 24, 256), vm(20, 24, 256), vm(24, 24, 256), vm(20, 24, 256),
            vm(2, 6, 16, 256), vm(2, 6, 16, 256), vm(2, 16, 8, 256), vm(2, 16, 8, 256), vm(4, 8, 256), vm(4, 8, 256),
            vm(20, 24, 256),
            vm(24, 24, 256), vm(20, 24, 256), vm(20, 24, 256), vm(16, 24, 256), vm(16, 24, 256), vm(26, 32, 256),
            vm(400, 128), vm(8, 16, 128), vm(3, 64, 128), vm(192, 128),
            vm(8, 16, 40, 128), vm(8, 56, 128), vm(8, 56, 128), vm(8, 56, 128), vm(5, 8, 8, 128),
            vm(8, 2, 8, 2, 8, 128), vm(2, 128, 128), vm(2, 128, 128),
            dma(3), dma(2), dma(2),
            dma(8), dma(8), dma(8), dma(8), dma(14), dma(14), dma(8), dma(8),
            pltpu.SemaphoreType.DMA, dma(8), dma(5), dma(5),
            pltpu.SemaphoreType.DMA, pltpu.SemaphoreType.DMA,
        ],
        compiler_params=pltpu.CompilerParams(
            collective_id=0, has_side_effects=True, vmem_limit_bytes=48 * 1024 * 1024
        ),
    )(guess)


def solution(mesh):
    spec = P(None, "tm", "gx", "gy", None)
    return jax.shard_map(local, mesh=mesh, in_specs=(spec,), out_specs=spec, check_vma=False)
```

```python
import jax
import jax.numpy as jnp
from jax import lax
from jax.experimental import pallas as pl
from jax.experimental.pallas import tpu as pltpu
from jax.sharding import PartitionSpec as P

DT = 0.01
HALF = 0.005
W = ((5.0 / 24.0, 1.0 / 3.0, -1.0 / 24.0), (-1.0 / 24.0, 1.0 / 3.0, 5.0 / 24.0))
OLD = (
    (DT * (W[0][0] - 0.5), DT * W[0][1], DT * W[0][2]),
    (DT * W[1][0], DT * (W[1][1] - 0.5), DT * W[1][2]),
)
MESH = pl.DeviceIdType.MESH
DIRS = ((1, 0), (-1, 0), (0, 1), (0, -1), (1, 1), (1, -1), (-1, 1), (-1, -1))
F32 = jnp.float32
HIGH = lax.Precision.HIGHEST


def dot(a, b):
    return jnp.dot(a, b, precision=HIGH, preferred_element_type=F32)


def around(c, low, high):
    rows, z = c.shape
    s = (low + high) + (pltpu.roll(c, 1, 0) + pltpu.roll(c, rows - 1, 0))
    s = s + (pltpu.roll(c, 1, 1) + pltpu.roll(c, z - 1, 1))
    return s - 6.0 * c


def around3(v):
    c = v[1:-1]
    rows, z = c.shape[1:]
    s = v[:-2] + v[2:] + pltpu.roll(c, 1, 1) + pltpu.roll(c, rows - 1, 1)
    s = s + pltpu.roll(c, 1, 2) + pltpu.roll(c, z - 1, 2)
    return s - 6.0 * c


def loop(count, body, group=1):
    def step(i, carry):
        base = jnp.minimum(group * i, count - group)
        for k in range(group):
            body(base + k)
        return carry

    lax.fori_loop(0, -(-count // group), step, 0)


def potential(src, mu, count, group):
    def body(x):
        c = src[x + 1]
        mu[x] = c * (c * c - 1.0) - around(c, src[x], src[x + 2])

    loop(count, body, group)


def crop(v):
    return pltpu.roll(v, 28, 0)[0:24]


def edge(h, d):
    return pl.ds(16 - h, h) if d > 0 else pl.ds(0, h)


def halo(h, d, at):
    return pl.ds(at - h, h) if d > 0 else pl.ds(at + 16, h)


CORNER = ((1, 0, 5), (4, 5, 2), (2, 8, 4), (3, 12, 3), (5, 15, 1))


def pack_corner(field, packed, k):
    dx, dy = DIRS[4 + k]
    for d, row, count in CORNER:
        x = 22 - d if dx > 0 else 5 + d
        y = 24 - count if dy > 0 else 8
        packed[..., k, row : row + count, :] = field[..., x, y : y + count, :]


def unpack_corner(field, packed, k):
    dx, dy = DIRS[4 + k]
    for d, row, count in CORNER:
        x = 6 - d if dx > 0 else 21 + d
        y = 8 - count if dy > 0 else 24
        field[..., x, y : y + count, :] = packed[..., k, row : row + count, :]


def kernel(
    g, out,
    zavg, zdup, ydup, raw, rsy, rry, rrc, q, w, mu, mu2,
    start, ssc, src_c, k0, k1, ksx, krx, ksy, kry, ksc, krc,
    u11, u12, u21, bb, usx, urx, usy, ury, usc, urc, u22,
    fs, f11, f21, j0, j1, wide,
    pair, co, cb, xext, gath, v0, v1, m0, seam, stage, back, half,
    in_s, st_s, st_r, raw_s, raw_r, k_s, k_r, s_s, s_r, u_s, u_r, g_s, g_r, x_s, x_r, b_s, b_r,
):
    n, a, b = lax.axis_index("tm"), lax.axis_index("gx"), lax.axis_index("gy")

    def at(dt, dx, dy):
        return (lax.rem(n + dt + 8, 8), lax.rem(a + dx + 4, 4), lax.rem(b + dy + 4, 4))

    barrier = pltpu.get_barrier_semaphore()
    for dx, dy in DIRS:
        pl.semaphore_signal(barrier, inc=1, device_id=at(0, dx, dy), device_id_type=MESH)
    for dt in range(1, 8):
        pl.semaphore_signal(barrier, inc=1, device_id=at(dt, 0, 0), device_id_type=MESH)

    block16 = (pl.ds(2, 16), pl.ds(8, 16))
    loads = [pltpu.make_async_copy(g.at[j, 0], raw.at[j, *block16], in_s.at[j]) for j in range(3)]
    for load in loads:
        load.start()

    def iota(shape, d):
        return lax.broadcasted_iota(jnp.int32, shape, d)

    zavg[...] = jnp.where(iota((256, 128), 0) // 2 == iota((256, 128), 1), 0.5, 0.0)
    zdup[...] = jnp.where(iota((128, 256), 0) == iota((128, 256), 1) // 2, 1.0, 0.0)
    r, k = iota((128, 64), 0), iota((128, 64), 1)
    ydup[...] = jnp.where(k == (r // 16) * 8 + lax.rem(r, 16) // 2, 1.0, 0.0)
    for load in loads:
        load.wait()
    for j in range(3):
        rsy[0, :, 2 * j : 2 * j + 2, :] = raw[j, 2:18, 22:24, :]
        rsy[1, :, 2 * j : 2 * j + 2, :] = raw[j, 2:18, 8:10, :]
    pl.semaphore_wait(barrier, 15)

    def send(src, dst, ss, rs, to):
        copy = pltpu.make_async_remote_copy(
            src_ref=src, dst_ref=dst, send_sem=ss, recv_sem=rs, device_id=to, device_id_type=MESH
        )
        copy.start()
        return copy

    along = [
        pltpu.make_async_remote_copy(
            src_ref=raw.at[2, pl.ds(2 + 8 * h, 8), pl.ds(8, 16)],
            dst_ref=start.at[pl.ds(6 + 8 * h, 8), pl.ds(8, 16)],
            send_sem=st_s.at[h], recv_sem=st_r.at[h], device_id=at(1, 0, 0), device_id_type=MESH,
        )
        for h in range(2)
    ]

    @pl.when(n < 7)
    def _():
        for copy in along:
            copy.start()

    raws = []
    for k, (dx, dy) in enumerate(DIRS):
        if dy == 0:
            src = raw.at[:, pl.ds(16, 2) if dx > 0 else pl.ds(2, 2), pl.ds(8, 16), :]
            dst = raw.at[:, halo(2, dx, 2), pl.ds(8, 16), :]
        elif dx == 0:
            src, dst = rsy.at[(1 - dy) // 2], rry.at[(1 - dy) // 2]
        else:
            src, dst = rsy.at[(1 - dy) // 2, edge(1, dx)], rrc.at[k - 4]
        raws.append(send(src, dst, raw_s.at[k], raw_r.at[k], at(0, dx, dy)))
    @pl.when(n == 0)
    def _():
        start[6:22, 8:24, :] = raw[0, 2:18, 8:24, :]

    starts = []
    for h in range(2):

        @pl.when(n > 0)
        def _():
            along[h].wait_recv()

        layers = pl.ds(6 + 8 * h, 8)
        for k, (dx, dy) in enumerate(DIRS):
            if dx == (1, -1)[h]:
                continue
            to, slot = at(0, dx, dy), k + 10 * h if dx == 0 else k
            if dx == 0:
                ys, yd = (pl.ds(16, 8), pl.ds(0, 8)) if dy > 0 else (pl.ds(8, 8), pl.ds(24, 8))
                src, dst = start.at[layers, ys], start.at[layers, yd]
            elif dy == 0:
                xs, xd = (pl.ds(16, 6), pl.ds(0, 6)) if dx > 0 else (pl.ds(6, 6), pl.ds(22, 6))
                src, dst = start.at[xs, pl.ds(8, 16)], start.at[xd, pl.ds(8, 16)]
            else:
                pack_corner(start, ssc, k - 4)
                src, dst = ssc.at[k - 4], src_c.at[k - 4]
            starts.append(send(src, dst, s_s.at[slot], s_r.at[slot], to))
    for copy in raws:
        copy.wait_recv()
    for s, row in ((0, 6), (1, 24)):
        for j in range(3):
            raw[j, 2:18, row : row + 2, :] = rry[s, :, 2 * j : 2 * j + 2, :]
            for e, x in ((0, 1), (2, 18)):
                raw[j, x, row : row + 2, :] = rrc[e + s, 0, 2 * j : 2 * j + 2, :]

    def mix(x):
        u = [raw[j, x] for j in range(3)]
        c = [v * (v * v - 1.0) for v in u]
        for i in range(2):
            q[i, x] = crop(OLD[i][0] * u[0] + OLD[i][1] * u[1] + OLD[i][2] * u[2])
            w[i, x] = crop(OLD[i][0] * c[0] + OLD[i][1] * c[1] + OLD[i][2] * c[2])

    def mix_potential(x):
        for i, m in ((0, mu), (1, mu2)):
            m[x] = w[i, x + 1] - around(q[i, x + 1], q[i, x], q[i, x + 2])

    def mix_force(x):
        k0[x + 4, 4:20, :] = around(mu[x + 1], mu[x], mu[x + 2])[4:20]
        k1[x + 2, 4:20, :] = around(mu2[x + 1], mu2[x], mu2[x + 2])[4:20]

    loop(20, mix, 5)
    loop(18, mix_potential, 6)
    loop(16, mix_force, 4)

    def wide_halo(p, r, xs, xr, ys, yr, cs, cr, ss, rs):
        for i in range(4):
            layers, near, row = pl.ds(4 + 4 * i, 4), pl.ds(2 + 4 * i, 4), 6 * i
            ys[0, :, row : row + 4, :] = p[layers, 16:20, :]
            ys[0, :, row + 4 : row + 6, :] = r[near, 18:20, :]
            ys[1, :, row : row + 4, :] = p[layers, 4:8, :]
            ys[1, :, row + 4 : row + 6, :] = r[near, 4:6, :]
        xs[0, 0:4] = p[16:20, 4:20, :]
        xs[0, 4:6] = r[16:18, 4:20, :]
        xs[1, 0:4] = p[4:8, 4:20, :]
        xs[1, 4:6] = r[2:4, 4:20, :]
        for k, (dx, dy) in enumerate(DIRS[4:]):
            for row, d, count in ((0, 1, 3), (3, 2, 2), (5, 3, 1)):
                x = 20 - d if dx > 0 else 3 + d
                y = 20 - count if dy > 0 else 4
                cs[k, row : row + count, :] = p[x, y : y + count, :]
            cs[k, 6:7, :] = r[17 if dx > 0 else 2, pl.ds(19 if dy > 0 else 4, 1), :]
        copies = []
        for k, (dx, dy) in enumerate(DIRS):
            s = (1 - dy) // 2
            if dy == 0:
                src, dst = xs.at[(1 - dx) // 2], xr.at[(1 - dx) // 2]
            elif dx == 0:
                src, dst = ys.at[s], yr.at[s]
            else:
                src, dst = cs.at[k - 4], cr.at[k - 4]
            copies.append(send(src, dst, ss.at[k], rs.at[k], at(0, dx, dy)))
        return copies

    def place(copies, p, r, xr, yr, cr):
        for copy in copies:
            copy.wait_recv()
        p[0:4, 4:20, :] = xr[0, 0:4]
        r[0:2, 4:20, :] = xr[0, 4:6]
        p[20:24, 4:20, :] = xr[1, 0:4]
        r[18:20, 4:20, :] = xr[1, 4:6]
        for s, low, near in ((0, 0, 2), (1, 20, 20)):
            for i in range(4):
                p[4 + 4 * i : 8 + 4 * i, low : low + 4, :] = yr[s, :, 6 * i : 6 * i + 4, :]
                r[2 + 4 * i : 6 + 4 * i, near : near + 2, :] = yr[s, :, 6 * i + 4 : 6 * i + 6, :]
        for k, (dx, dy) in enumerate(DIRS[4:]):
            for row, d, count in ((0, 1, 3), (3, 2, 2), (5, 3, 1)):
                x = 4 - d if dx > 0 else 19 + d
                y = 4 - count if dy > 0 else 20
                p[x, y : y + count, :] = cr[k, row : row + count, :]
            r[1 if dx > 0 else 18, pl.ds(3 if dy > 0 else 20, 1), :] = cr[k, 6:7, :]

    ks = wide_halo(k0, k1, ksx, krx, ksy, kry, ksc, krc, k_s, k_r)

    for copy in starts:
        copy.wait_recv()
    for k in range(4):
        unpack_corner(start, src_c, k)
    potential(start, wide, 26, 9)
    place(ks, k0, k1, krx, kry, krc)

    def first(x):
        f = around(wide[x + 1], wide[x], wide[x + 2])
        fs[x] = crop(f)
        u11[x] = crop(start[x + 2] + HALF * f) + k0[x]

    loop(24, first, 8)
    potential(u11, mu, 22, 8)

    def second(x):
        f = around(mu[x + 1], mu[x], mu[x + 2])
        f11[x] = f
        u12[x] = u11[x + 2] + HALF * f + k1[x]

    loop(20, second, 10)
    potential(u12, mu, 18, 9)

    def third(x):
        f2 = around(mu[x + 1], mu[x], mu[x + 2])
        f0, f1 = fs[x + 4], f11[x + 2]
        new = crop(start[x + 6]) + DT * (W[0][0] * f0 + W[0][1] * f1 + W[0][2] * f2)
        u21[x + 4, 4:20, :] = new[4:20]
        bb[x + 2, 4:20, :] = (OLD[1][0] * f0 + OLD[1][1] * f1 + OLD[1][2] * f2)[4:20]

    loop(16, third, 8)
    us = wide_halo(u21, bb, usx, urx, usy, ury, usc, urc, u_s, u_r)

    def average(layers, rows):
        both = [(layers[2 * i] + layers[2 * i + 1]) * 0.25 for i in range(len(layers) // 2)]
        pair[0 : len(both) * rows, :] = dot(jnp.concatenate(both, axis=0), zavg[...])

    def coarse_rows(first_row, count):
        return pair[pl.ds(first_row, count, stride=2), :] + pair[pl.ds(first_row + 1, count, stride=2), :]

    def bricks(rows, offset, skip):
        return jnp.concatenate([coarse_rows(rows * (i + skip) + offset, 8) for i in range(8)], axis=0)

    def coarse_force(rows, offset):
        v = jnp.concatenate([coarse_rows(rows * i + offset, 16) for i in range(12)], axis=0)
        v = v.reshape(12, 16, 128)
        c = v[1:-1]
        m = c * (c * c - 1.0) - 0.25 * around3(v)
        co[...] = 0.25 * around3(m)
        return jnp.concatenate([co[i, 2:10, :] for i in range(8)], axis=0)

    average([start[x + 2] for x in range(24)], 32)
    cb[0] = bricks(32, 8, 2)
    g0 = coarse_force(32, 4)
    place(us, u21, bb, urx, ury, urc)
    potential(u21, mu, 22, 8)

    def fourth(x):
        f = around(mu[x + 1], mu[x], mu[x + 2])
        f21[x] = f
        u22[x] = u21[x + 2] + HALF * f + bb[x]

    loop(20, fourth, 10)
    potential(u22, mu, 18, 9)

    def fifth(x):
        f2 = around(mu[x + 1], mu[x], mu[x + 2])
        f0, f1 = fs[x + 4], f21[x + 2]
        j0[x] = DT * (W[0][0] * f0 + W[0][1] * f1 + W[0][2] * f2)
        j1[x] = DT * (W[1][0] * f0 + W[1][1] * f1 + W[1][2] * f2)

    loop(16, fifth, 8)
    average([u21[x] for x in range(24)], 24)
    cb[1] = bricks(24, 4, 2)
    g1 = coarse_force(24, 0)
    average([j[x] for j in (j0, j1) for x in range(16)], 24)
    part0, part1 = bricks(24, 4, 0), bricks(24, 4, 8)
    part0 = part0 + jnp.where(n == 0, cb[0], -HALF * g0)
    part1 = part1 - HALF * g1
    turned = jnp.transpose(jnp.concatenate([part0, part1], axis=0))
    xext[32:160, :] = turned
    xext[0:32, :] = turned[96:128]
    xext[160:192, :] = turned[0:32]

    block = a * 4 + b

    def chain_device(p):
        t, x = lax.rem(p, 8), 2 * (p // 8)
        return (t, x, lax.rem(x + t // 4 + t, 4))

    is_chain = jnp.logical_and(lax.rem(a, 2) == 0, b == lax.rem(a + n // 4 + n, 4))
    me = n + 8 * (a // 2)
    mine = jnp.where(is_chain, me, -1)
    late = lax.rem(n, 4) // 2

    for c, (low, length) in enumerate(((0, 40), (8, 24))):

        @pl.when(late == c)
        def _():
            def part(p):
                src = xext.at[pl.ds(pl.multiple_of(8 * p + 16 + low, 8), length), :]
                return src, gath.at[n, block, pl.ds(low, length), :]

            for p in range(16):

                @pl.when(p != mine)
                def _():
                    send(*part(p), g_s, g_r.at[n], chain_device(p))

            @pl.when(is_chain)
            def _():
                pltpu.make_async_copy(*part(me), g_r.at[n]).start()

    average([u22[x + 2] for x in range(16)], 24)
    cb[2] = bricks(24, 4, 0)

    lane = lax.broadcasted_iota(jnp.int32, (8, 128), 1)
    inner = lane & 7

    def chain_lap(ref, lo, hi, put):
        for r in range(lo, hi, 8):
            c = [ref[t, r : r + 8, :] for t in range(8)]
            turn = lambda by: [pltpu.roll(v, by % 128, 1) for v in c]
            xp, xm, yp, ym, yu, yd = (turn(by) for by in (-8, 8, -1, 1, 7, -7))
            for t in range(8):
                o, up, down = (t + 4) % 8, t // 4 * 4 + (t + 1) % 4, t // 4 * 4 + (t + 3) % 4
                s = jnp.where(lane < 120, xp[t], xp[o]) + jnp.where(lane >= 8, xm[t], xm[o])
                s = s + (jnp.where(inner < 7, yp[t], yu[up]) + jnp.where(inner > 0, ym[t], yd[down]))
                s = s + (ref[t, r + 1 : r + 9, :] + ref[t, r - 1 : r + 7, :])
                put(t, r, c[t], 0.25 * (s - 6.0 * c[t]))

    @pl.when(is_chain)
    def _():
        v0[...] = jnp.zeros_like(v0)

        def sweep(src, dst, m, first, inside, outside):
            def one(t, r, u, l):
                m0[t, r : r + 8, :] = u * (u * u - 1.0) - l

            def two(t, r, u, f):
                x, y = t // 4, t % 4
                rows = pl.ds(r - 8, 8)
                e, o = gath[m, 8 * x + y, rows, :], gath[m, 8 * x + 4 + y, rows, :]
                if first:
                    part = jnp.where(lane < 64, e, pltpu.roll(o, 64, 1))
                else:
                    part = jnp.where(lane < 64, pltpu.roll(e, 64, 1), o)
                dst[t, r : r + 8, :] = src[t, r : r + 8, :] + HALF * f + part

            chain_lap(src, *inside, one)
            chain_lap(m0, *outside, two)

        full, part, core = (8, 48), (16, 40), (24, 32)
        spans = (
            (full, full, full, full),
            (full, full, full, part),
            (part, part, part, part),
            (part, part, part, core),
        )

        def other(d, k):
            p = lax.rem(me + d + 16, 16)
            return pltpu.make_async_remote_copy(
                src_ref=stage.at[3, 0, :, 1], dst_ref=seam.at[k], send_sem=x_s.at[k], recv_sem=x_r.at[k],
                device_id=chain_device(p), device_id_type=MESH,
            )

        seams = [other(d, k) for k, d in ((0, 2), (1, 1), (3, -1), (4, -2))]

        def scatter(m):
            for d in range(16):
                to = lax.rem(block + d, 16)
                x, y = to // 4, lax.rem(to, 4)
                src = stage.at[m, lax.rem(x, 2), (x // 2) * 4 + y]
                dst = back.at[:, pl.ds(pl.multiple_of(8 * me, 8), 8), :]
                if d > 0:
                    send(src, dst, b_s, b_r, (m, x, y))
                else:

                    @pl.when(m != n)
                    def _():
                        send(src, dst, b_s, b_r, (m, x, y))

                    @pl.when(m == n)
                    def _():
                        pltpu.make_async_copy(src, dst, b_r).start()

        def phase(h):
            @pl.when(h == 1)
            def _():
                for copy in seams:
                    copy.start()
                scatter(3)
                for copy in seams:
                    copy.wait()
                for k in (0, 1, 3, 4):
                    v0[:, 8 + 8 * k : 16 + 8 * k, :] = seam[k]

            for i in range(4):
                m = 4 * h + i
                low, length = ((0, 40), (8, 24))[i // 2]
                whole = gath.at[m, :, pl.ds(low, length), :]
                pltpu.make_async_copy(whole, whole, g_r.at[m]).wait()
                begin = [v0[t, 24:32, :] for t in range(8)]
                sweep(v0, v1, m, True, *spans[i][:2])
                for t in range(8):
                    middle = v1[t, 24:32, :]
                    stage[m, 0, t, 0] = jnp.where(lane < 64, begin[t], pltpu.roll(middle, 64, 1))
                    stage[m, 1, t, 0] = jnp.where(lane < 64, pltpu.roll(begin[t], 64, 1), middle)
                sweep(v1, v0, m, False, *spans[i][2:])
                stage[m, 0, :, 1] = v0[:, 24:32, :]
                stage[m, 1, :, 1] = v0[:, 24:32, :]

                if i < 3:
                    scatter(m)
                else:

                    @pl.when(h == 1)
                    def _():
                        scatter(m)

        loop(2, phase)

    pltpu.make_async_copy(back, back, b_r).wait()
    half[0] = jnp.transpose(back[0])
    half[1] = jnp.transpose(back[1])
    own_half = pl.ds(pl.multiple_of(64 * lax.rem(a, 2), 64), 64)
    changes = [half[0, 0:64] - cb[0], half[0, 64:128] - cb[1], half[1, own_half] - cb[2]]
    changes[0] = jnp.where(n == 0, 0.0, changes[0])
    tall = dot(ydup[...], jnp.concatenate(changes, axis=1))
    fines = dot(jnp.concatenate([tall[:, 128 * j : 128 * j + 128] for j in range(3)], axis=0), zdup[...])
    for j in range(3):
        fine = fines[128 * j : 128 * j + 128]
        for i in range(8):
            add = fine[16 * i : 16 * i + 16]
            for x in (2 * i, 2 * i + 1):
                if j == 0:
                    node = start[x + 6, 8:24, :]
                elif j == 1:
                    node = u21[x + 4, 4:20, :]
                else:
                    node = u22[x + 2, 4:20, :]
                out[j, 0, x] = node + add

    @pl.when(n < 7)
    def _():
        for copy in along:
            copy.wait_send()

    for copy in raws + ks + starts + us:
        copy.wait_send()
    for c, (low, length) in enumerate(((0, 40), (8, 24))):

        @pl.when(late == c)
        def _():
            @pl.when(is_chain)
            def _():
                sent = gath.at[0, 0:15, pl.ds(low, length), :]
                pltpu.make_async_copy(sent, sent, g_s).wait()

            @pl.when(jnp.logical_not(is_chain))
            def _():
                sent = gath.at[0, :, pl.ds(low, length), :]
                pltpu.make_async_copy(sent, sent, g_s).wait()

    @pl.when(is_chain)
    def _():
        sent = stage.at[0, 0, 0:7]
        pltpu.make_async_copy(sent, sent, b_s).wait()
        sent = stage.at[0, 1]
        pltpu.make_async_copy(sent, sent, b_s).wait()
        for m in range(1, 8):
            pltpu.make_async_copy(stage.at[m], stage.at[m], b_s).wait()


def local(guess):
    vm = lambda *s: pltpu.VMEM(s, F32)
    dma = lambda *s: pltpu.SemaphoreType.DMA(s)
    vspec = pl.BlockSpec(memory_space=pltpu.VMEM)
    return pl.pallas_call(
        kernel,
        out_shape=jax.ShapeDtypeStruct(guess.shape, F32),
        in_specs=[pl.BlockSpec(memory_space=pl.ANY)],
        out_specs=vspec,
        scratch_shapes=[
            vm(256, 128), vm(128, 256), vm(128, 64),
            vm(3, 20, 32, 256), vm(2, 16, 8, 256), vm(2, 16, 8, 256), vm(4, 1, 8, 256),
            vm(2, 20, 24, 256), vm(2, 20, 24, 256), vm(22, 24, 256), vm(22, 24, 256),
            vm(28, 32, 256), vm(4, 16, 256), vm(4, 16, 256), vm(24, 24, 256), vm(20, 24, 256),
            vm(2, 6, 16, 256), vm(2, 6, 16, 256), vm(2, 4, 24, 256), vm(2, 4, 24, 256), vm(4, 8, 256), vm(4, 8, 256),
            vm(24, 24, 256), vm(20, 24, 256), vm(24, 24, 256), vm(20, 24, 256),
            vm(2, 6, 16, 256), vm(2, 6, 16, 256), vm(2, 4, 24, 256), vm(2, 4, 24, 256), vm(4, 8, 256), vm(4, 8, 256),
            vm(20, 24, 256),
            vm(24, 24, 256), vm(20, 24, 256), vm(20, 24, 256), vm(16, 24, 256), vm(16, 24, 256), vm(26, 32, 256),
            vm(400, 128), vm(8, 16, 128), vm(3, 64, 128), vm(192, 128),
            vm(8, 16, 40, 128), vm(8, 56, 128), vm(8, 56, 128), vm(8, 56, 128), vm(5, 8, 8, 128),
            vm(8, 2, 8, 2, 8, 128), vm(2, 128, 128), vm(2, 128, 128),
            dma(3), dma(2), dma(2),
            dma(8), dma(8), dma(8), dma(8), dma(14), dma(14), dma(8), dma(8),
            pltpu.SemaphoreType.DMA, dma(8), dma(5), dma(5),
            pltpu.SemaphoreType.DMA, pltpu.SemaphoreType.DMA,
        ],
        compiler_params=pltpu.CompilerParams(
            collective_id=0, has_side_effects=True, vmem_limit_bytes=48 * 1024 * 1024
        ),
    )(guess)


def solution(mesh):
    spec = P(None, "tm", "gx", "gy", None)
    return jax.shard_map(local, mesh=mesh, in_specs=(spec,), out_specs=spec, check_vma=False)
```

```python
import jax
import jax.numpy as jnp
from jax import lax
from jax.experimental import pallas as pl
from jax.experimental.pallas import tpu as pltpu
from jax.sharding import PartitionSpec as P

DT = 0.01
HALF = 0.005
W = ((5.0 / 24.0, 1.0 / 3.0, -1.0 / 24.0), (-1.0 / 24.0, 1.0 / 3.0, 5.0 / 24.0))
OLD = (
    (DT * (W[0][0] - 0.5), DT * W[0][1], DT * W[0][2]),
    (DT * W[1][0], DT * (W[1][1] - 0.5), DT * W[1][2]),
)
MESH = pl.DeviceIdType.MESH
DIRS = ((1, 0), (-1, 0), (0, 1), (0, -1), (1, 1), (1, -1), (-1, 1), (-1, -1))
F32 = jnp.float32
HIGH = lax.Precision.HIGHEST


def dot(a, b):
    return jnp.dot(a, b, precision=HIGH, preferred_element_type=F32)


def around(c, low, high):
    rows, z = c.shape
    s = (low + high) + (pltpu.roll(c, 1, 0) + pltpu.roll(c, rows - 1, 0))
    s = s + (pltpu.roll(c, 1, 1) + pltpu.roll(c, z - 1, 1))
    return s - 6.0 * c


def around3(v):
    c = v[1:-1]
    rows, z = c.shape[1:]
    s = v[:-2] + v[2:] + pltpu.roll(c, 1, 1) + pltpu.roll(c, rows - 1, 1)
    s = s + pltpu.roll(c, 1, 2) + pltpu.roll(c, z - 1, 2)
    return s - 6.0 * c


def loop(count, body, group=1):
    def step(i, carry):
        base = jnp.minimum(group * i, count - group)
        for k in range(group):
            body(base + k)
        return carry

    lax.fori_loop(0, -(-count // group), step, 0)


def potential(src, mu, count, group):
    def body(x):
        c = src[x + 1]
        mu[x] = c * (c * c - 1.0) - around(c, src[x], src[x + 2])

    loop(count, body, group)


def crop(v):
    return pltpu.roll(v, 28, 0)[0:24]


def edge(h, d):
    return pl.ds(16 - h, h) if d > 0 else pl.ds(0, h)


def halo(h, d, at):
    return pl.ds(at - h, h) if d > 0 else pl.ds(at + 16, h)


CORNER = ((1, 0, 5), (4, 5, 2), (2, 8, 4), (3, 12, 3), (5, 15, 1))


def pack_corner(field, packed, k):
    dx, dy = DIRS[4 + k]
    for d, row, count in CORNER:
        x = 22 - d if dx > 0 else 5 + d
        y = 24 - count if dy > 0 else 8
        packed[..., k, row : row + count, :] = field[..., x, y : y + count, :]


def unpack_corner(field, packed, k):
    dx, dy = DIRS[4 + k]
    for d, row, count in CORNER:
        x = 6 - d if dx > 0 else 21 + d
        y = 8 - count if dy > 0 else 24
        field[..., x, y : y + count, :] = packed[..., k, row : row + count, :]


def kernel(
    g, out,
    zavg, zdup, ydup, raw, rsy, rry, rrc, q, w, mu, mu2,
    start, ssc, src_c, k0, k1, ksx, krx, ksy, kry, ksc, krc,
    u11, u12, u21, bb, usx, urx, usy, ury, usc, urc, u22,
    fs, f11, f21, j0, j1, wide,
    pair, co, cb, xext, gath, v0, v1, m0, seam, stage, back, half,
    in_s, st_s, st_r, raw_s, raw_r, k_s, k_r, s_s, s_r, u_s, u_r, g_s, g_r, x_s, x_r, b_s, b_r,
):
    n, a, b = lax.axis_index("tm"), lax.axis_index("gx"), lax.axis_index("gy")

    def at(dt, dx, dy):
        return (lax.rem(n + dt + 8, 8), lax.rem(a + dx + 4, 4), lax.rem(b + dy + 4, 4))

    barrier = pltpu.get_barrier_semaphore()
    for dx, dy in DIRS:
        pl.semaphore_signal(barrier, inc=1, device_id=at(0, dx, dy), device_id_type=MESH)
    for dt in range(1, 8):
        pl.semaphore_signal(barrier, inc=1, device_id=at(dt, 0, 0), device_id_type=MESH)

    block16 = (pl.ds(2, 16), pl.ds(8, 16))
    loads = [pltpu.make_async_copy(g.at[j, 0], raw.at[j, *block16], in_s.at[j]) for j in range(3)]
    for load in loads:
        load.start()

    def iota(shape, d):
        return lax.broadcasted_iota(jnp.int32, shape, d)

    zavg[...] = jnp.where(iota((256, 128), 0) // 2 == iota((256, 128), 1), 0.5, 0.0)
    zdup[...] = jnp.where(iota((128, 256), 0) == iota((128, 256), 1) // 2, 1.0, 0.0)
    r, k = iota((128, 64), 0), iota((128, 64), 1)
    ydup[...] = jnp.where(k == (r // 16) * 8 + lax.rem(r, 16) // 2, 1.0, 0.0)
    for load in loads:
        load.wait()
    for j in range(3):
        rsy[0, :, 2 * j : 2 * j + 2, :] = raw[j, 2:18, 22:24, :]
        rsy[1, :, 2 * j : 2 * j + 2, :] = raw[j, 2:18, 8:10, :]
    pl.semaphore_wait(barrier, 15)

    def send(src, dst, ss, rs, to):
        copy = pltpu.make_async_remote_copy(
            src_ref=src, dst_ref=dst, send_sem=ss, recv_sem=rs, device_id=to, device_id_type=MESH
        )
        copy.start()
        return copy

    along = [
        pltpu.make_async_remote_copy(
            src_ref=raw.at[2, pl.ds(2 + 8 * h, 8), pl.ds(8, 16)],
            dst_ref=start.at[pl.ds(6 + 8 * h, 8), pl.ds(8, 16)],
            send_sem=st_s.at[h], recv_sem=st_r.at[h], device_id=at(1, 0, 0), device_id_type=MESH,
        )
        for h in range(2)
    ]

    @pl.when(n < 7)
    def _():
        for copy in along:
            copy.start()

    raws = []
    for k, (dx, dy) in enumerate(DIRS):
        if dy == 0:
            src = raw.at[:, pl.ds(16, 2) if dx > 0 else pl.ds(2, 2), pl.ds(8, 16), :]
            dst = raw.at[:, halo(2, dx, 2), pl.ds(8, 16), :]
        elif dx == 0:
            src, dst = rsy.at[(1 - dy) // 2], rry.at[(1 - dy) // 2]
        else:
            src, dst = rsy.at[(1 - dy) // 2, edge(1, dx)], rrc.at[k - 4]
        raws.append(send(src, dst, raw_s.at[k], raw_r.at[k], at(0, dx, dy)))
    @pl.when(n == 0)
    def _():
        start[6:22, 8:24, :] = raw[0, 2:18, 8:24, :]

    starts = []
    for h in range(2):

        @pl.when(n > 0)
        def _():
            along[h].wait_recv()

        layers = pl.ds(6 + 8 * h, 8)
        for k, (dx, dy) in enumerate(DIRS):
            if dx == (1, -1)[h]:
                continue
            to, slot = at(0, dx, dy), k + 10 * h if dx == 0 else k
            if dx == 0:
                ys, yd = (pl.ds(16, 8), pl.ds(0, 8)) if dy > 0 else (pl.ds(8, 8), pl.ds(24, 8))
                src, dst = start.at[layers, ys], start.at[layers, yd]
            elif dy == 0:
                xs, xd = (pl.ds(16, 6), pl.ds(0, 6)) if dx > 0 else (pl.ds(6, 6), pl.ds(22, 6))
                src, dst = start.at[xs, pl.ds(8, 16)], start.at[xd, pl.ds(8, 16)]
            else:
                pack_corner(start, ssc, k - 4)
                src, dst = ssc.at[k - 4], src_c.at[k - 4]
            starts.append(send(src, dst, s_s.at[slot], s_r.at[slot], to))
    for copy in raws:
        copy.wait_recv()
    for s, row in ((0, 6), (1, 24)):
        for j in range(3):
            raw[j, 2:18, row : row + 2, :] = rry[s, :, 2 * j : 2 * j + 2, :]
            for e, x in ((0, 1), (2, 18)):
                raw[j, x, row : row + 2, :] = rrc[e + s, 0, 2 * j : 2 * j + 2, :]

    def mix(x):
        u = [raw[j, x] for j in range(3)]
        c = [v * (v * v - 1.0) for v in u]
        for i in range(2):
            q[i, x] = crop(OLD[i][0] * u[0] + OLD[i][1] * u[1] + OLD[i][2] * u[2])
            w[i, x] = crop(OLD[i][0] * c[0] + OLD[i][1] * c[1] + OLD[i][2] * c[2])

    def mix_potential(x):
        for i, m in ((0, mu), (1, mu2)):
            m[x] = w[i, x + 1] - around(q[i, x + 1], q[i, x], q[i, x + 2])

    def mix_force(x):
        k0[x + 4, 4:20, :] = around(mu[x + 1], mu[x], mu[x + 2])[4:20]
        k1[x + 2, 4:20, :] = around(mu2[x + 1], mu2[x], mu2[x + 2])[4:20]

    loop(20, mix, 5)
    loop(18, mix_potential, 6)
    loop(16, mix_force, 4)

    def wide_halo(p, r, xs, xr, ys, yr, cs, cr, ss, rs):
        for i in range(4):
            layers, near, row = pl.ds(4 + 4 * i, 4), pl.ds(2 + 4 * i, 4), 6 * i
            ys[0, :, row : row + 4, :] = p[layers, 16:20, :]
            ys[0, :, row + 4 : row + 6, :] = r[near, 18:20, :]
            ys[1, :, row : row + 4, :] = p[layers, 4:8, :]
            ys[1, :, row + 4 : row + 6, :] = r[near, 4:6, :]
        xs[0, 0:4] = p[16:20, 4:20, :]
        xs[0, 4:6] = r[16:18, 4:20, :]
        xs[1, 0:4] = p[4:8, 4:20, :]
        xs[1, 4:6] = r[2:4, 4:20, :]
        for k, (dx, dy) in enumerate(DIRS[4:]):
            for row, d, count in ((0, 1, 3), (3, 2, 2), (5, 3, 1)):
                x = 20 - d if dx > 0 else 3 + d
                y = 20 - count if dy > 0 else 4
                cs[k, row : row + count, :] = p[x, y : y + count, :]
            cs[k, 6:7, :] = r[17 if dx > 0 else 2, pl.ds(19 if dy > 0 else 4, 1), :]
        copies = []
        for k, (dx, dy) in enumerate(DIRS):
            s = (1 - dy) // 2
            if dy == 0:
                src, dst = xs.at[(1 - dx) // 2], xr.at[(1 - dx) // 2]
            elif dx == 0:
                src, dst = ys.at[s], yr.at[s]
            else:
                src, dst = cs.at[k - 4], cr.at[k - 4]
            copies.append(send(src, dst, ss.at[k], rs.at[k], at(0, dx, dy)))
        return copies

    def place(copies, p, r, xr, yr, cr):
        for copy in copies:
            copy.wait_recv()
        p[0:4, 4:20, :] = xr[0, 0:4]
        r[0:2, 4:20, :] = xr[0, 4:6]
        p[20:24, 4:20, :] = xr[1, 0:4]
        r[18:20, 4:20, :] = xr[1, 4:6]
        for s, low, near in ((0, 0, 2), (1, 20, 20)):
            for i in range(4):
                p[4 + 4 * i : 8 + 4 * i, low : low + 4, :] = yr[s, :, 6 * i : 6 * i + 4, :]
                r[2 + 4 * i : 6 + 4 * i, near : near + 2, :] = yr[s, :, 6 * i + 4 : 6 * i + 6, :]
        for k, (dx, dy) in enumerate(DIRS[4:]):
            for row, d, count in ((0, 1, 3), (3, 2, 2), (5, 3, 1)):
                x = 4 - d if dx > 0 else 19 + d
                y = 4 - count if dy > 0 else 20
                p[x, y : y + count, :] = cr[k, row : row + count, :]
            r[1 if dx > 0 else 18, pl.ds(3 if dy > 0 else 20, 1), :] = cr[k, 6:7, :]

    ks = wide_halo(k0, k1, ksx, krx, ksy, kry, ksc, krc, k_s, k_r)

    for copy in starts:
        copy.wait_recv()
    for k in range(4):
        unpack_corner(start, src_c, k)
    potential(start, wide, 26, 9)
    place(ks, k0, k1, krx, kry, krc)

    def first(x):
        f = around(wide[x + 1], wide[x], wide[x + 2])
        fs[x] = crop(f)
        u11[x] = crop(start[x + 2] + HALF * f) + k0[x]

    loop(24, first, 8)
    potential(u11, mu, 22, 8)

    def second(x):
        f = around(mu[x + 1], mu[x], mu[x + 2])
        f11[x] = f
        u12[x] = u11[x + 2] + HALF * f + k1[x]

    loop(20, second, 10)
    potential(u12, mu, 18, 9)

    def third(x):
        f2 = around(mu[x + 1], mu[x], mu[x + 2])
        f0, f1 = fs[x + 4], f11[x + 2]
        new = crop(start[x + 6]) + DT * (W[0][0] * f0 + W[0][1] * f1 + W[0][2] * f2)
        u21[x + 4, 4:20, :] = new[4:20]
        bb[x + 2, 4:20, :] = (OLD[1][0] * f0 + OLD[1][1] * f1 + OLD[1][2] * f2)[4:20]

    loop(16, third, 8)
    us = wide_halo(u21, bb, usx, urx, usy, ury, usc, urc, u_s, u_r)

    def average(layers, rows):
        both = [(layers[2 * i] + layers[2 * i + 1]) * 0.25 for i in range(len(layers) // 2)]
        pair[0 : len(both) * rows, :] = dot(jnp.concatenate(both, axis=0), zavg[...])

    def coarse_rows(first_row, count):
        return pair[pl.ds(first_row, count, stride=2), :] + pair[pl.ds(first_row + 1, count, stride=2), :]

    def bricks(rows, offset, skip):
        return jnp.concatenate([coarse_rows(rows * (i + skip) + offset, 8) for i in range(8)], axis=0)

    def coarse_force(rows, offset):
        v = jnp.concatenate([coarse_rows(rows * i + offset, 16) for i in range(12)], axis=0)
        v = v.reshape(12, 16, 128)
        c = v[1:-1]
        m = c * (c * c - 1.0) - 0.25 * around3(v)
        co[...] = 0.25 * around3(m)
        return jnp.concatenate([co[i, 2:10, :] for i in range(8)], axis=0)

    average([start[x + 2] for x in range(24)], 32)
    cb[0] = bricks(32, 8, 2)
    g0 = coarse_force(32, 4)
    place(us, u21, bb, urx, ury, urc)
    potential(u21, mu, 22, 8)

    def fourth(x):
        f = around(mu[x + 1], mu[x], mu[x + 2])
        f21[x] = f
        u22[x] = u21[x + 2] + HALF * f + bb[x]

    loop(20, fourth, 10)
    potential(u22, mu, 18, 9)

    def fifth(x):
        f2 = around(mu[x + 1], mu[x], mu[x + 2])
        f0, f1 = fs[x + 4], f21[x + 2]
        j0[x] = DT * (W[0][0] * f0 + W[0][1] * f1 + W[0][2] * f2)
        j1[x] = DT * (W[1][0] * f0 + W[1][1] * f1 + W[1][2] * f2)

    loop(16, fifth, 8)
    average([u21[x] for x in range(24)], 24)
    cb[1] = bricks(24, 4, 2)
    g1 = coarse_force(24, 0)
    average([j[x] for j in (j0, j1) for x in range(16)], 24)
    part0, part1 = bricks(24, 4, 0), bricks(24, 4, 8)
    part0 = part0 + jnp.where(n == 0, cb[0], -HALF * g0)
    part1 = part1 - HALF * g1
    turned = jnp.transpose(jnp.concatenate([part0, part1], axis=0))
    xext[32:160, :] = turned
    xext[0:32, :] = turned[96:128]
    xext[160:192, :] = turned[0:32]

    block = a * 4 + b

    def chain_device(p):
        t, x = lax.rem(p, 8), 2 * (p // 8)
        return (t, x, lax.rem(x + t // 4 + t, 4))

    is_chain = jnp.logical_and(lax.rem(a, 2) == 0, b == lax.rem(a + n // 4 + n, 4))
    me = n + 8 * (a // 2)
    mine = jnp.where(is_chain, me, -1)
    late = lax.rem(n, 4) // 2

    for c, (low, length) in enumerate(((0, 40), (8, 24))):

        @pl.when(late == c)
        def _():
            def part(p):
                src = xext.at[pl.ds(pl.multiple_of(8 * p + 16 + low, 8), length), :]
                return src, gath.at[n, block, pl.ds(low, length), :]

            for p in range(16):

                @pl.when(p != mine)
                def _():
                    send(*part(p), g_s, g_r.at[n], chain_device(p))

            @pl.when(is_chain)
            def _():
                pltpu.make_async_copy(*part(me), g_r.at[n]).start()

    average([u22[x + 2] for x in range(16)], 24)
    cb[2] = bricks(24, 4, 0)

    lane = lax.broadcasted_iota(jnp.int32, (8, 128), 1)
    inner = lane & 7

    def chain_lap(ref, lo, hi, put):
        for r in range(lo, hi, 8):
            c = [ref[t, r : r + 8, :] for t in range(8)]
            turn = lambda by: [pltpu.roll(v, by % 128, 1) for v in c]
            xp, xm, yp, ym, yu, yd = (turn(by) for by in (-8, 8, -1, 1, 7, -7))
            for t in range(8):
                o, up, down = (t + 4) % 8, t // 4 * 4 + (t + 1) % 4, t // 4 * 4 + (t + 3) % 4
                s = jnp.where(lane < 120, xp[t], xp[o]) + jnp.where(lane >= 8, xm[t], xm[o])
                s = s + (jnp.where(inner < 7, yp[t], yu[up]) + jnp.where(inner > 0, ym[t], yd[down]))
                s = s + (ref[t, r + 1 : r + 9, :] + ref[t, r - 1 : r + 7, :])
                put(t, r, c[t], 0.25 * (s - 6.0 * c[t]))

    @pl.when(is_chain)
    def _():
        v0[...] = jnp.zeros_like(v0)

        def two_bricks(m, t, r):
            x, y = t // 4, t % 4
            rows = pl.ds(r - 8, 8)
            return gath[m, 8 * x + y, rows, :], gath[m, 8 * x + 4 + y, rows, :]

        def first_part(m, t, r):
            e, o = two_bricks(m, t, r)
            return jnp.where(lane < 64, e, pltpu.roll(o, 64, 1))

        def second_part(m, t, r):
            e, o = two_bricks(m, t, r)
            return jnp.where(lane < 64, pltpu.roll(e, 64, 1), o)

        def sweep(src, dst, m, first, inside, outside):
            def one(t, r, u, l):
                m0[t, r : r + 8, :] = u * (u * u - 1.0) - l

            def two(t, r, u, f):
                part = first_part(m, t, r) if first else second_part(m, t, r)
                dst[t, r : r + 8, :] = src[t, r : r + 8, :] + HALF * f + part

            chain_lap(src, *inside, one)
            chain_lap(m0, *outside, two)

        full, part, core = (8, 48), (16, 40), (24, 32)
        spans = (
            (full, full, full, full),
            (full, full, full, part),
            (part, part, part, part),
            (part, part, part, core),
        )

        def other(d, k):
            p = lax.rem(me + d + 16, 16)
            return pltpu.make_async_remote_copy(
                src_ref=stage.at[3, 0, :, 1], dst_ref=seam.at[k], send_sem=x_s.at[k], recv_sem=x_r.at[k],
                device_id=chain_device(p), device_id_type=MESH,
            )

        seams = [other(d, k) for k, d in ((0, 2), (1, 1), (3, -1), (4, -2))]

        def scatter(m):
            for d in range(16):
                to = lax.rem(block + d, 16)
                x, y = to // 4, lax.rem(to, 4)
                src = stage.at[m, lax.rem(x, 2), (x // 2) * 4 + y]
                dst = back.at[:, pl.ds(pl.multiple_of(8 * me, 8), 8), :]
                if d > 0:
                    send(src, dst, b_s, b_r, (m, x, y))
                else:

                    @pl.when(m != n)
                    def _():
                        send(src, dst, b_s, b_r, (m, x, y))

                    @pl.when(m == n)
                    def _():
                        pltpu.make_async_copy(src, dst, b_r).start()

        def phase(h):
            @pl.when(h == 1)
            def _():
                for copy in seams:
                    copy.start()
                scatter(3)
                for copy in seams:
                    copy.wait()
                for k in (0, 1, 3, 4):
                    v0[:, 8 + 8 * k : 16 + 8 * k, :] = seam[k]

            for i in range(4):
                m = 4 * h + i
                low, length = ((0, 40), (8, 24))[i // 2]
                whole = gath.at[m, :, pl.ds(low, length), :]
                pltpu.make_async_copy(whole, whole, g_r.at[m]).wait()
                begin = [v0[t, 24:32, :] for t in range(8)]
                if i > 0:
                    sweep(v0, v1, m, True, *spans[i][:2])
                else:

                    @pl.when(h == 0)
                    def _():
                        for t in range(8):
                            for r in range(*full, 8):
                                v1[t, r : r + 8, :] = first_part(m, t, r)

                    @pl.when(h == 1)
                    def _():
                        sweep(v0, v1, m, True, *spans[0][:2])

                for t in range(8):
                    middle = v1[t, 24:32, :]
                    stage[m, 0, t, 0] = jnp.where(lane < 64, begin[t], pltpu.roll(middle, 64, 1))
                    stage[m, 1, t, 0] = jnp.where(lane < 64, pltpu.roll(begin[t], 64, 1), middle)
                sweep(v1, v0, m, False, *spans[i][2:])
                stage[m, 0, :, 1] = v0[:, 24:32, :]
                stage[m, 1, :, 1] = v0[:, 24:32, :]

                if i < 3:
                    scatter(m)
                else:

                    @pl.when(h == 1)
                    def _():
                        scatter(m)

        loop(2, phase)

    pltpu.make_async_copy(back, back, b_r).wait()
    half[0] = jnp.transpose(back[0])
    half[1] = jnp.transpose(back[1])
    own_half = pl.ds(pl.multiple_of(64 * lax.rem(a, 2), 64), 64)
    changes = [half[0, 0:64] - cb[0], half[0, 64:128] - cb[1], half[1, own_half] - cb[2]]
    changes[0] = jnp.where(n == 0, 0.0, changes[0])
    tall = dot(ydup[...], jnp.concatenate(changes, axis=1))
    fines = dot(jnp.concatenate([tall[:, 128 * j : 128 * j + 128] for j in range(3)], axis=0), zdup[...])
    for j in range(3):
        fine = fines[128 * j : 128 * j + 128]
        for i in range(8):
            add = fine[16 * i : 16 * i + 16]
            for x in (2 * i, 2 * i + 1):
                if j == 0:
                    node = start[x + 6, 8:24, :]
                elif j == 1:
                    node = u21[x + 4, 4:20, :]
                else:
                    node = u22[x + 2, 4:20, :]
                out[j, 0, x] = node + add

    @pl.when(n < 7)
    def _():
        for copy in along:
            copy.wait_send()

    for copy in raws + ks + starts + us:
        copy.wait_send()
    for c, (low, length) in enumerate(((0, 40), (8, 24))):

        @pl.when(late == c)
        def _():
            @pl.when(is_chain)
            def _():
                sent = gath.at[0, 0:15, pl.ds(low, length), :]
                pltpu.make_async_copy(sent, sent, g_s).wait()

            @pl.when(jnp.logical_not(is_chain))
            def _():
                sent = gath.at[0, :, pl.ds(low, length), :]
                pltpu.make_async_copy(sent, sent, g_s).wait()

    @pl.when(is_chain)
    def _():
        sent = stage.at[0, 0, 0:7]
        pltpu.make_async_copy(sent, sent, b_s).wait()
        sent = stage.at[0, 1]
        pltpu.make_async_copy(sent, sent, b_s).wait()
        for m in range(1, 8):
            pltpu.make_async_copy(stage.at[m], stage.at[m], b_s).wait()


def local(guess):
    vm = lambda *s: pltpu.VMEM(s, F32)
    dma = lambda *s: pltpu.SemaphoreType.DMA(s)
    vspec = pl.BlockSpec(memory_space=pltpu.VMEM)
    return pl.pallas_call(
        kernel,
        out_shape=jax.ShapeDtypeStruct(guess.shape, F32),
        in_specs=[pl.BlockSpec(memory_space=pl.ANY)],
        out_specs=vspec,
        scratch_shapes=[
            vm(256, 128), vm(128, 256), vm(128, 64),
            vm(3, 20, 32, 256), vm(2, 16, 8, 256), vm(2, 16, 8, 256), vm(4, 1, 8, 256),
            vm(2, 20, 24, 256), vm(2, 20, 24, 256), vm(22, 24, 256), vm(22, 24, 256),
            vm(28, 32, 256), vm(4, 16, 256), vm(4, 16, 256), vm(24, 24, 256), vm(20, 24, 256),
            vm(2, 6, 16, 256), vm(2, 6, 16, 256), vm(2, 4, 24, 256), vm(2, 4, 24, 256), vm(4, 8, 256), vm(4, 8, 256),
            vm(24, 24, 256), vm(20, 24, 256), vm(24, 24, 256), vm(20, 24, 256),
            vm(2, 6, 16, 256), vm(2, 6, 16, 256), vm(2, 4, 24, 256), vm(2, 4, 24, 256), vm(4, 8, 256), vm(4, 8, 256),
            vm(20, 24, 256),
            vm(24, 24, 256), vm(20, 24, 256), vm(20, 24, 256), vm(16, 24, 256), vm(16, 24, 256), vm(26, 32, 256),
            vm(400, 128), vm(8, 16, 128), vm(3, 64, 128), vm(192, 128),
            vm(8, 16, 40, 128), vm(8, 56, 128), vm(8, 56, 128), vm(8, 56, 128), vm(5, 8, 8, 128),
            vm(8, 2, 8, 2, 8, 128), vm(2, 128, 128), vm(2, 128, 128),
            dma(3), dma(2), dma(2),
            dma(8), dma(8), dma(8), dma(8), dma(14), dma(14), dma(8), dma(8),
            pltpu.SemaphoreType.DMA, dma(8), dma(5), dma(5),
            pltpu.SemaphoreType.DMA, pltpu.SemaphoreType.DMA,
        ],
        compiler_params=pltpu.CompilerParams(
            collective_id=0, has_side_effects=True, vmem_limit_bytes=48 * 1024 * 1024
        ),
    )(guess)


def solution(mesh):
    spec = P(None, "tm", "gx", "gy", None)
    return jax.shard_map(local, mesh=mesh, in_specs=(spec,), out_specs=spec, check_vma=False)
```
